32 devices in a mesh: groups: 2 (over y), var: 8 (over z, x), tm: 2 (over core).
Axes of the slice: x: 2, y: 2, z: 4, core: 2. Of those that a mesh axis runs over, the one named last changes fastest.
Arguments:
- series: bfloat16 [4, 512, 4096], P('groups', 'var', 'tm'), parts along dimension 0, may hold values from -71 to 71
- target: float32 [4, 512, 720], P('groups', 'var', 'tm'), parts along dimension 0, may hold values from -71 to 71
- w_embed: bfloat16 [4096, 512], P('tm'), may hold values from -0.09375 to 0.09375
- w_query: bfloat16 [512, 256], P(None, 'tm'), may hold values from -0.25 to 0.25
- w_key: bfloat16 [512, 256], P(None, 'tm'), may hold values from -0.25 to 0.25
- w_value: bfloat16 [512, 256], P(None, 'tm'), may hold values from -0.25 to 0.25
- w_out: bfloat16 [256, 512], P('tm'), may hold values from -0.375 to 0.375
- norm_gain: float32 [512], replicated, may hold values from 0.5 to 1.5
- w_head: bfloat16 [512, 720], P(None, 'tm'), may hold values from -0.25 to 0.25
Outputs:
- predicted_values: float32 [4, 512, 720], P('groups', 'var', 'tm'), parts along dimension 0
- question_projection_derivative: float32 [1024, 256], P('groups', 'tm'), parts along dimension 0
- final_projection_derivative: float32 [512, 512], P(('groups', 'tm')), parts along dimension 0
- layernorm_scale_derivative: float32 [1024], P('groups'), parts along dimension 0
- future_readout_derivative: float32 [1024, 720], P('groups', 'tm'), parts along dimension 0
The draws below stay inside these ranges and needn't reach their ends.
There are 2 independent parts, one for each index of `groups`. The reference program is written for one: setup_inputs(seed, part) draws one part's arguments, and reference() takes and returns one part's arrays. A program takes and returns all parts, laid end to end along the dimension named above; an argument that names none is the same for every part. Nothing has to cross between parts.
All inputs are finite; a program needn't handle non-finite values.
Results may differ from the reference program's by a relative error of at most 0.015.
Values may be sent and summed in bfloat16 or wider, within the bound.
A program may use at most 128 MiB of HBM per device.

```python
import math
import jax
import jax.numpy as jnp
from jax import lax

D = 512
HEADS = 4
HEAD_DIM = 64
LOOK = 4096
HOR = 720
SAMPLES = 2
SERIES = 512


def series_law(key):
    level_key, scale_key = jax.random.split(jax.random.fold_in(key, 7))
    levels = jax.random.uniform(level_key, (SAMPLES, SERIES, 1), jnp.float32, -3.0, 3.0)
    scales = jnp.exp(jax.random.uniform(scale_key, (SAMPLES, SERIES, 1), jnp.float32, 0.0, math.log(10.0)))
    return (levels, scales)


def draw_series(key, part):
    levels, scales = series_law(key)
    noise_key = jax.random.fold_in(jax.random.fold_in(key, 19), 0)
    noise = jnp.clip(jax.random.normal(noise_key, (SAMPLES, SERIES, LOOK), jnp.float32), -4.0, 4.0)
    return (scales * (levels + noise)).astype(jnp.bfloat16)


def draw_target(key, part):
    levels, scales = series_law(key)
    noise_key = jax.random.fold_in(jax.random.fold_in(key, 23), 0)
    noise = jnp.clip(jax.random.normal(noise_key, (SAMPLES, SERIES, HOR), jnp.float32), -4.0, 4.0)
    return (scales * (levels + noise)).astype(jnp.float32)


def block_levels(stream_key, extent, cuts, least, top_value):
    factor_of, own = 1.0, jax.random.fold_in(stream_key, 6)
    for dim, shards_of in cuts:
        steps = jnp.exp(jax.random.uniform(jax.random.fold_in(own, dim), (shards_of,), jnp.float32, least / len(cuts), top_value / len(cuts)))
        factor_of = factor_of * jnp.repeat(steps, extent[dim] // shards_of).reshape([-1 if axis == dim else 1 for axis in range(len(extent))])
    return factor_of


def bell_draw(own_key, shape, scale, reach, cuts=(), kind=jnp.bfloat16):
    result = scale * jax.random.normal(own_key, shape, jnp.float32)
    if cuts:
        result = result * block_levels(own_key, shape, cuts, -0.22, 0.18)
    return jnp.clip(result, -reach, reach).astype(kind)


def setup_inputs(seed: int = 0, part: int = 0) -> dict:
    key_list = jax.random.split(jax.random.key(seed), 10)
    own_keys = jax.random.split(jax.random.fold_in(key_list[9], part), 10)
    return {
        "series": draw_series(jax.random.fold_in(jax.random.fold_in(key_list[9], part), 71), part),
        "target": draw_target(jax.random.fold_in(jax.random.fold_in(key_list[9], part), 71), part),
        "w_embed": bell_draw(key_list[2], (LOOK, D), LOOK ** -0.5, 0.09375, ((0, 2),)),
        "w_query": bell_draw(key_list[3], (D, HEADS * HEAD_DIM), D ** -0.5, 0.25, ((1, 2),)),
        "w_key": bell_draw(key_list[4], (D, HEADS * HEAD_DIM), D ** -0.5, 0.25, ((1, 2),)),
        "w_value": bell_draw(key_list[5], (D, HEADS * HEAD_DIM), D ** -0.5, 0.25, ((1, 2),)),
        "w_out": bell_draw(key_list[6], (HEADS * HEAD_DIM, D), (HEADS * HEAD_DIM) ** -0.5, 0.375, ((0, 2),)),
        "norm_gain": jnp.clip(1.0 + 0.1 * jax.random.normal(key_list[7], (D,), jnp.float32), 0.5, 1.5),
        "w_head": bell_draw(key_list[8], (D, HOR), D ** -0.5, 0.25, ((1, 2),)),
    }


epsilon = 1e-05

def rounded(tensor_in):
    return lax.optimization_barrier(tensor_in.astype(jnp.bfloat16)).astype(jnp.float32)

def product(form, left, right):
    return jnp.einsum(form, left.astype(jnp.float32), right.astype(jnp.float32), precision=lax.Precision.HIGHEST)

def reference(series, target, w_embed, w_query, w_key, w_value, w_out, norm_gain, w_head):
    series_f = series.astype(jnp.float32)
    instance_average = lax.optimization_barrier(jnp.mean(series_f, axis=2))
    centered = series_f - instance_average[:, :, None]
    instance_dispersion = jnp.sqrt(lax.optimization_barrier(jnp.mean(centered * centered, axis=2)) + epsilon)
    normed = rounded(centered / instance_dispersion[:, :, None])
    hidden = rounded(product('svl,ld->svd', normed, w_embed))
    queries = rounded(product('svd,da->sva', hidden, w_query))
    key_rows = rounded(product('svd,da->sva', hidden, w_key))
    value_rows = rounded(product('svd,da->sva', hidden, w_value))
    width = math.gcd(SERIES, 512)
    blocks = SERIES // width
    score_scale = HEAD_DIM ** (-0.5)
    heads_shape = (SAMPLES, SERIES, HEADS, HEAD_DIM)
    query_heads = queries.reshape(heads_shape)
    key_heads = key_rows.reshape(heads_shape)
    value_heads = value_rows.reshape(heads_shape)
    contexts = []
    sums_all = []
    for sample in range(SAMPLES):
        key_part = key_heads[sample]
        value_part = value_heads[sample]

        def forward_block(query_block, key_part=key_part, value_part=value_part):
            scores = product('nhe,mhe->hnm', query_block, key_part) * score_scale
            powers = jnp.exp(scores)
            row_sums = lax.optimization_barrier(jnp.sum(powers, axis=2))
            summed = product('hnm,mhe->nhe', rounded(powers), value_part)
            return (summed / jnp.transpose(row_sums)[:, :, None], jnp.transpose(row_sums))
        block_context, block_sums = lax.map(forward_block, query_heads[sample].reshape(blocks, width, HEADS, HEAD_DIM))
        contexts.append(block_context.reshape(SERIES, HEADS * HEAD_DIM))
        sums_all.append(block_sums.reshape(SERIES, HEADS))
    context = jnp.stack(contexts)
    row_totals = jnp.stack(sums_all)
    context_low = rounded(context)
    mixing = product('sva,ad->svd', context_low, w_out)
    residual = hidden + mixing
    shifted = residual - lax.optimization_barrier(jnp.mean(residual, axis=2, keepdims=True))
    norm_root = jnp.sqrt(lax.optimization_barrier(jnp.mean(shifted * shifted, axis=2, keepdims=True)) + epsilon)
    unit_rows = shifted / norm_root
    normal_out = rounded(unit_rows * norm_gain)
    future_rescaler = product('svd,dh->svh', normal_out, w_head)
    predicted_values = future_rescaler * instance_dispersion[:, :, None] + instance_average[:, :, None]
    errors = future_rescaler - (target - instance_average[:, :, None]) / instance_dispersion[:, :, None]
    grad_horizon = rounded(errors * (2.0 / (SAMPLES * HOR)))
    future_readout_derivative = product('svd,svh->dh', normal_out, grad_horizon)
    grad_normal = product('svh,dh->svd', grad_horizon, w_head)
    layernorm_scale_derivative = lax.optimization_barrier(jnp.sum(grad_normal * unit_rows, axis=(0, 1)))
    grad_unit = grad_normal * norm_gain
    grad_mix = rounded((grad_unit - lax.optimization_barrier(jnp.mean(grad_unit, axis=2, keepdims=True)) - unit_rows * lax.optimization_barrier(jnp.mean(grad_unit * unit_rows, axis=2, keepdims=True))) / norm_root)
    final_projection_derivative = product('sva,svd->ad', context_low, grad_mix)
    grad_context = product('svd,ad->sva', grad_mix, w_out)
    grads_all = []
    for sample in range(SAMPLES):
        key_part = key_heads[sample]
        value_part = value_heads[sample]

        def backward_block(pieces, key_part=key_part, value_part=value_part):
            query_block, context_block, grad_block, sum_block = pieces
            scores = product('nhe,mhe->hnm', query_block, key_part) * score_scale
            weights = jnp.exp(scores) / jnp.transpose(sum_block)[:, :, None]
            grad_weights = product('nhe,mhe->hnm', rounded(grad_block), value_part)
            row_dots = lax.optimization_barrier(jnp.sum(grad_block * context_block, axis=2))
            grad_scores = rounded(weights * (grad_weights - jnp.transpose(row_dots)[:, :, None]))
            return product('hnm,mhe->nhe', grad_scores, key_part) * score_scale
        pieces = (query_heads[sample].reshape(blocks, width, HEADS, HEAD_DIM), context[sample].reshape(blocks, width, HEADS, HEAD_DIM), grad_context[sample].reshape(blocks, width, HEADS, HEAD_DIM), row_totals[sample].reshape(blocks, width, HEADS))
        grads_all.append(lax.map(backward_block, pieces).reshape(SERIES, HEADS * HEAD_DIM))
    grad_query = rounded(jnp.stack(grads_all))
    question_projection_derivative = product('svd,sva->da', hidden, grad_query)
    return (predicted_values, question_projection_derivative, final_projection_derivative, layernorm_scale_derivative, future_readout_derivative)
```

```python
import functools

import jax
import jax.numpy as jnp
from jax import lax
from jax.experimental import pallas as pl
from jax.experimental.pallas import tpu as pltpu
from jax.sharding import PartitionSpec as P

HEAD_DIM = 64
EPSILON = 1e-05
MESH = pl.DeviceIdType.MESH
F32, BF16 = jnp.float32, jnp.bfloat16


def dot(a, b):
    return jnp.dot(a, b, preferred_element_type=F32)


def dot_nt(a, b):
    return lax.dot_general(a, b, (((1,), (1,)), ((), ())), preferred_element_type=F32)


def dot_tn(a, b):
    return lax.dot_general(a, b, (((0,), (0,)), ((), ())), preferred_element_type=F32)


def repeat(count, body, carry):
    if count == 1:
        return body(0, carry)
    return lax.fori_loop(0, count, body, carry)


def kernel(
    n, reduce_here, key_chunk,
    series, target, w_embed, w_query, w_key, w_value, w_out, norm_gain, w_head,
    pred_out, query_out, final_out, gain_out, head_out,
    pack, got, wq, wk, wv, wo, wh, tg, hid, keys, values, powers, pred_half, pred_got,
    no2, gh_all, gh2, gm2, cl_all, cl2, gq_src, gq_all, gains, gain_mine,
    head_src, head_slots, head_full, out_src, out_slots, out_full,
    pair_send, pair_recv, hid_send, hid_recv, gq_send, gq_recv, gain_send, gain_recv,
    hr_send, hr_recv, ha_send, ha_recv, or_send, or_recv, oa_send, oa_recv,
):
    me = lax.axis_index("var")
    t = lax.axis_index("tm")
    other = 1 - t
    my_id = me * 2 + t
    rows = series.shape[1]
    steps = series.shape[2]
    horizon = 2 * target.shape[2]
    samples = series.shape[0]
    heads_half = w_query.shape[1] // HEAD_DIM
    heads = 2 * heads_half
    block = pl.ds(pl.multiple_of(me * rows, rows), rows)

    def to_pair(index, src, dst):
        return pltpu.make_async_remote_copy(
            src_ref=src, dst_ref=dst, send_sem=pair_send.at[index], recv_sem=pair_recv.at[index],
            device_id={"var": me, "tm": other}, device_id_type=MESH,
        )

    def spread(src_of, dst_of, send, recv):
        def go(i, carry):
            peer = lax.rem(me + 1 + i, n)
            pltpu.make_async_remote_copy(
                src_ref=src_of(peer), dst_ref=dst_of(me), send_sem=send.at[peer], recv_sem=recv.at[me],
                device_id={"var": peer, "tm": t}, device_id_type=MESH,
            ).start()
            return carry
        lax.fori_loop(0, n - 1, go, 0)

    def settle(src_of, dst_of, send, recv, which):
        def go(i, carry):
            peer = lax.rem(me + 1 + i, n)
            copy = pltpu.make_async_remote_copy(
                src_ref=src_of(peer), dst_ref=dst_of(peer), send_sem=send.at[peer], recv_sem=recv.at[peer],
                device_id={"var": peer, "tm": t}, device_id_type=MESH,
            )
            if which == "recv":
                copy.wait_recv()
            else:
                copy.wait_send()
            return carry
        lax.fori_loop(0, n - 1, go, 0)

    def everyone(body):
        def go(i, carry):
            where = lax.rem(my_id + 1 + i, 2 * n)
            body(where, where // 2, lax.rem(where, 2))
            return carry
        lax.fori_loop(0, 2 * n - 1, go, 0)

    barrier = pltpu.get_barrier_semaphore()

    def greet(where, p, q):
        pl.semaphore_signal(barrier, inc=1, device_id={"var": p, "tm": q}, device_id_type=MESH)
    everyone(greet)

    ones = jnp.ones((16, steps), BF16)
    sums = dot(ones, w_embed[...])[:8]
    for s in range(samples):
        x = series[s].astype(F32)
        mean = jnp.mean(x, axis=1, keepdims=True)
        centred = x - mean
        spread_sum = jnp.sum(centred * centred, axis=1, keepdims=True)
        width = w_embed.shape[1]
        pack[s, :rows, :width] = dot(centred.astype(BF16), w_embed[...])
        pack[s, :rows, width:width + 128] = jnp.broadcast_to(mean, (rows, 128))
        pack[s, :rows, width + 128:] = jnp.broadcast_to(spread_sum, (rows, 128))
        pack[s, rows:, :width] = sums
        pack[s, rows:, width:] = jnp.zeros((8, 256), F32)

    pl.semaphore_wait(barrier, 2 * n - 1)
    first = to_pair(0, pack.at[other], got)
    first.start()
    weight_copies = [
        to_pair(1, w_query, wq.at[t]),
        to_pair(2, w_key, wk.at[t]),
        to_pair(3, w_value, wv.at[t]),
        to_pair(4, w_out, wo.at[t]),
        to_pair(5, w_head, wh.at[t]),
        to_pair(6, target.at[other], tg.at[t]),
    ]
    for copy in weight_copies:
        copy.start()
    wq[t] = w_query[...]
    wk[t] = w_key[...]
    wv[t] = w_value[...]
    wo[t] = w_out[...]
    wh[t] = w_head[...]
    tg[t] = target[t]
    first.wait()

    width = w_embed.shape[1]
    mean_a, mean_b = pack[t, :rows, width:width + 1], got[:rows, width:width + 1]
    sq_a, sq_b = pack[t, :rows, width + 128:width + 129], got[:rows, width + 128:width + 129]
    center = (mean_a + mean_b) * 0.5
    half_gap = (mean_a - mean_b) * 0.5
    deviation = jnp.sqrt((sq_a + sq_b) * (1.0 / (2 * steps)) + half_gap * half_gap + EPSILON)
    sums_a, sums_b = pack[t, rows:rows + 1, :width], got[rows:rows + 1, :width]
    hidden = (
        (pack[t, :rows, :width] + got[:rows, :width] + half_gap * (sums_a - sums_b)) / deviation
    ).astype(BF16)
    hid[t, block, :] = hidden

    mine = hid.at[t, block, :]
    hid_from = lambda p: hid.at[t, pl.ds(pl.multiple_of(p * rows, rows), rows), :]
    spread(lambda p: mine, hid_from, hid_send, hid_recv)

    for copy in weight_copies:
        copy.wait()
    queries = jnp.concatenate([dot(hidden, wq[0]), dot(hidden, wq[1])], axis=1).astype(BF16)
    queries = (queries.astype(F32) * HEAD_DIM ** (-0.5)).astype(BF16)
    q_heads = [queries[:, h * HEAD_DIM:(h + 1) * HEAD_DIM] for h in range(heads)]

    settle(lambda p: mine, hid_from, hid_send, hid_recv, "recv")
    relay = to_pair(7, hid.at[t], hid.at[t])
    relay.start()

    chunks = n * rows // key_chunk

    def chunk_rows(c):
        if chunks == 1:
            return pl.ds(0, key_chunk)
        return pl.ds(pl.multiple_of(c * key_chunk, key_chunk), key_chunk)

    def forward(c, carry):
        totals, summed = carry
        at = chunk_rows(c)
        h_rows = hid[t, at, :]
        key_rows = jnp.concatenate([dot(h_rows, wk[0]), dot(h_rows, wk[1])], axis=1).astype(BF16)
        value_rows = jnp.concatenate([dot(h_rows, wv[0]), dot(h_rows, wv[1])], axis=1).astype(BF16)
        keys[at, :] = key_rows
        values[at, :] = value_rows
        new_totals, new_summed = [], []
        for h in range(heads):
            cols = slice(h * HEAD_DIM, (h + 1) * HEAD_DIM)
            p = jnp.exp(dot_nt(q_heads[h], key_rows[:, cols]))
            powers[h, c] = p
            new_totals.append(totals[h] + jnp.sum(p, axis=1, keepdims=True))
            new_summed.append(summed[h] + dot(p.astype(BF16), value_rows[:, cols]))
        return tuple(new_totals), tuple(new_summed)

    zero = (
        tuple(jnp.zeros((rows, 1), F32) for _ in range(heads)),
        tuple(jnp.zeros((rows, HEAD_DIM), F32) for _ in range(heads)),
    )
    totals, summed = repeat(chunks, forward, zero)
    context = jnp.concatenate([summed[h] / totals[h] for h in range(heads)], axis=1)
    context_low = context.astype(BF16)
    half = context.shape[1] // 2
    w_out_all = wo[...].reshape(2 * half, width)
    residual = hidden.astype(F32) + dot(context_low, w_out_all)
    shifted = residual - jnp.mean(residual, axis=1, keepdims=True)
    norm_root = jnp.sqrt(jnp.mean(shifted * shifted, axis=1, keepdims=True) + EPSILON)
    unit_rows = shifted / norm_root
    gain = norm_gain[...]
    normal_out = (unit_rows * gain).astype(BF16)
    no2[t] = normal_out
    send_no = to_pair(8, no2.at[t], no2.at[t])
    send_no.start()
    grad_normal = jnp.zeros((rows, width), F32)
    for h in range(2):
        horizon_norm = dot(normal_out, wh[h])
        pred_half[h] = horizon_norm * deviation + center
        errors = horizon_norm - (tg[h] - center) / deviation
        grad_h = (errors * (2.0 / (samples * horizon))).astype(BF16)
        gh_all[h] = grad_h
        grad_normal += dot_nt(grad_h, wh[h])
    send_gh = to_pair(9, gh_all.at[other], gh2.at[t])
    send_gh.start()
    send_pred = to_pair(10, pred_half.at[other], pred_got)
    send_pred.start()
    gh2[t] = gh_all[t]
    pred_out[t] = pred_half[t]

    gain_mine[...] = jnp.sum(grad_normal * unit_rows, axis=0, keepdims=True)
    grad_unit = grad_normal * gain
    grad_mix = (
        (
            grad_unit
            - jnp.mean(grad_unit, axis=1, keepdims=True)
            - unit_rows * jnp.mean(grad_unit * unit_rows, axis=1, keepdims=True)
        )
        / norm_root
    ).astype(BF16)
    gm2[t] = grad_mix
    for h in range(2):
        cl_all[h] = context_low[:, h * half:(h + 1) * half]
    send_gm = to_pair(11, gm2.at[t], gm2.at[t])
    send_gm.start()
    send_cl = to_pair(12, cl_all.at[other], cl2.at[t])
    send_cl.start()
    cl2[t] = cl_all[t]

    def gain_copy(where, p, q, slot):
        return pltpu.make_async_remote_copy(
            src_ref=gain_mine, dst_ref=gains.at[slot], send_sem=gain_send.at[where], recv_sem=gain_recv.at[slot],
            device_id={"var": p, "tm": q}, device_id_type=MESH,
        )

    if reduce_here:
        gains[my_id] = gain_mine[...]
        everyone(lambda where, p, q: gain_copy(where, p, q, my_id).start())
    else:
        gain_out[...] = gain_mine[...]

    grad_context = dot_nt(grad_mix, w_out_all)
    gc_heads, row_dots, scales = [], [], []
    for h in range(heads):
        cols = slice(h * HEAD_DIM, (h + 1) * HEAD_DIM)
        gc_heads.append(grad_context[:, cols].astype(BF16))
        row_dots.append(jnp.sum(grad_context[:, cols] * context[:, cols], axis=1, keepdims=True))
        scales.append(1.0 / totals[h])

    def backward(c, carry):
        at = chunk_rows(c)
        key_rows, value_rows = keys[at, :], values[at, :]
        results = []
        for h in range(heads):
            cols = slice(h * HEAD_DIM, (h + 1) * HEAD_DIM)
            grad_weights = dot_nt(gc_heads[h], value_rows[:, cols])
            grad_scores = (powers[h, c] * scales[h] * (grad_weights - row_dots[h])).astype(BF16)
            results.append(carry[h] + dot(grad_scores, key_rows[:, cols]))
        return tuple(results)

    grads = repeat(chunks, backward, zero[1])
    grad_query = (jnp.concatenate(grads, axis=1) * HEAD_DIM ** (-0.5)).astype(BF16)
    for h in range(2):
        gq_src[h] = grad_query[:, h * half:(h + 1) * half]

    def gq_copy(where, p, q, slot):
        return pltpu.make_async_remote_copy(
            src_ref=gq_src.at[q],
            dst_ref=gq_all.at[lax.rem(slot, 2), pl.ds(pl.multiple_of((slot // 2) * rows, rows), rows), :],
            send_sem=gq_send.at[where], recv_sem=gq_recv.at[slot],
            device_id={"var": p, "tm": q}, device_id_type=MESH,
        )

    everyone(lambda where, p, q: gq_copy(where, p, q, my_id).start())
    gq_all[t, block, :] = gq_src[t]

    send_no.wait()
    send_gh.wait()
    head_term = dot_tn(no2[...].reshape(samples * rows, width), gh2[...].reshape(samples * rows, horizon // 2))
    if reduce_here:
        head_src[...] = head_term.astype(BF16).reshape(head_src.shape)
        spread(lambda p: head_src.at[p], lambda p: head_slots.at[p], hr_send, hr_recv)
    else:
        head_out[...] = head_term
    send_gm.wait()
    send_cl.wait()
    out_term = dot_tn(cl2[...].reshape(samples * rows, half), gm2[...].reshape(samples * rows, width))
    if reduce_here:
        out_src[...] = out_term.astype(BF16).reshape(out_src.shape)
        spread(lambda p: out_src.at[p], lambda p: out_slots.at[p], or_send, or_recv)
        head_slots[me] = head_src[me]
        out_slots[me] = out_src[me]
    else:
        final_out[...] = out_term
    send_pred.wait()
    pred_out[other] = pred_got[...]

    if reduce_here:
        settle(lambda p: head_src.at[p], lambda p: head_slots.at[p], hr_send, hr_recv, "recv")
        head_full[me] = jnp.sum(head_slots[...].astype(F32), axis=0).astype(BF16)
        spread(lambda p: head_full.at[me], lambda p: head_full.at[p], ha_send, ha_recv)
        settle(lambda p: out_src.at[p], lambda p: out_slots.at[p], or_send, or_recv, "recv")
        out_full[me] = jnp.sum(out_slots[...].astype(F32), axis=0).astype(BF16)
        spread(lambda p: out_full.at[me], lambda p: out_full.at[p], oa_send, oa_recv)

    relay.wait()
    everyone(lambda where, p, q: gq_copy(where, p, q, where).wait_recv())
    query_out[...] = dot_tn(
        hid[...].reshape(samples * n * rows, width), gq_all[...].reshape(samples * n * rows, half)
    )
    if reduce_here:
        everyone(lambda where, p, q: gain_copy(where, p, q, where).wait_recv())
        gain_out[...] = jnp.sum(gains[...], axis=0)
        settle(lambda p: head_full.at[me], lambda p: head_full.at[p], ha_send, ha_recv, "recv")
        head_out[...] = head_full[...].astype(F32).reshape(head_out.shape)
        settle(lambda p: out_full.at[me], lambda p: out_full.at[p], oa_send, oa_recv, "recv")
        final_out[...] = out_full[...].astype(F32).reshape(final_out.shape)

    settle(lambda p: mine, hid_from, hid_send, hid_recv, "send")
    everyone(lambda where, p, q: gq_copy(where, p, q, my_id).wait_send())
    if reduce_here:
        everyone(lambda where, p, q: gain_copy(where, p, q, my_id).wait_send())
        settle(lambda p: head_src.at[p], lambda p: head_slots.at[p], hr_send, hr_recv, "send")
        settle(lambda p: out_src.at[p], lambda p: out_slots.at[p], or_send, or_recv, "send")
        settle(lambda p: head_full.at[me], lambda p: head_full.at[p], ha_send, ha_recv, "send")
        settle(lambda p: out_full.at[me], lambda p: out_full.at[p], oa_send, oa_recv, "send")


def solution(mesh):
    n = mesh.shape["var"]

    def per_device(series, target, w_embed, w_query, w_key, w_value, w_out, norm_gain, w_head):
        samples, rows, steps = series.shape
        width = w_embed.shape[1]
        half = w_query.shape[1]
        hor = target.shape[2]
        heads = 2 * half // HEAD_DIM
        key_chunk = min(512, n * rows)
        chunks = n * rows // key_chunk
        reduce_here = width % (16 * n) == 0 and half % (16 * n) == 0
        cuts = n if reduce_here else 1
        v = pltpu.VMEM
        dma = pltpu.SemaphoreType.DMA
        outs = pl.pallas_call(
            functools.partial(kernel, n, reduce_here, key_chunk),
            out_shape=(
                jax.ShapeDtypeStruct((samples, rows, hor), F32),
                jax.ShapeDtypeStruct((width, half), F32),
                jax.ShapeDtypeStruct((half, width), F32),
                jax.ShapeDtypeStruct((1, width), F32),
                jax.ShapeDtypeStruct((width, hor), F32),
            ),
            in_specs=[pl.BlockSpec(memory_space=pltpu.VMEM)] * 9,
            out_specs=[pl.BlockSpec(memory_space=pltpu.VMEM)] * 5,
            scratch_shapes=[
                v((samples, rows + 8, width + 256), F32),
                v((rows + 8, width + 256), F32),
                v((2, width, half), BF16),
                v((2, width, half), BF16),
                v((2, width, half), BF16),
                v((2, half, width), BF16),
                v((2, width, hor), BF16),
                v((2, rows, hor), F32),
                v((samples, n * rows, width), BF16),
                v((n * rows, 2 * half), BF16),
                v((n * rows, 2 * half), BF16),
                v((heads, chunks, rows, key_chunk), F32),
                v((2, rows, hor), F32),
                v((rows, hor), F32),
                v((samples, rows, width), BF16),
                v((2, rows, hor), BF16),
                v((samples, rows, hor), BF16),
                v((samples, rows, width), BF16),
                v((2, rows, half), BF16),
                v((samples, rows, half), BF16),
                v((2, rows, half), BF16),
                v((samples, n * rows, half), BF16),
                v((2 * cuts, 1, width), F32),
                v((1, width), F32),
                v((cuts, width // cuts, hor), BF16),
                v((cuts, width // cuts, hor), BF16),
                v((cuts, width // cuts, hor), BF16),
                v((cuts, half // cuts, width), BF16),
                v((cuts, half // cuts, width), BF16),
                v((cuts, half // cuts, width), BF16),
                dma((13,)), dma((13,)),
                dma((n,)), dma((n,)),
                dma((2 * n,)), dma((2 * n,)),
                dma((2 * n,)), dma((2 * n,)),
                dma((n,)), dma((n,)), dma((n,)), dma((n,)),
                dma((n,)), dma((n,)), dma((n,)), dma((n,)),
            ],
            compiler_params=pltpu.CompilerParams(
                collective_id=0,
                has_side_effects=True,
                vmem_limit_bytes=(40 if n <= 16 else 62) * 1024 * 1024,
            ),
        )(series, target, w_embed, w_query, w_key, w_value, w_out, norm_gain.reshape(1, width), w_head)
        pred, query, final, gain, head = outs
        if not reduce_here:
            query_same = query
            final, gain, head = lax.psum((final, gain, head), "var")
            gain = lax.psum(gain, "tm")
            query = query_same
        return pred, query, final, gain.reshape(width), head

    in_specs = (
        P("groups", "var", "tm"),
        P("groups", "var", "tm"),
        P("tm", None),
        P(None, "tm"),
        P(None, "tm"),
        P(None, "tm"),
        P("tm", None),
        P(),
        P(None, "tm"),
    )
    out_specs = (
        P("groups", "var", "tm"),
        P("groups", "tm"),
        P(("groups", "tm"), None),
        P("groups"),
        P("groups", "tm"),
    )
    return jax.shard_map(
        per_device, mesh=mesh, in_specs=in_specs, out_specs=out_specs, check_vma=False
    )
```

```python
import functools

import jax
import jax.numpy as jnp
from jax import lax
from jax.experimental import pallas as pl
from jax.experimental.pallas import tpu as pltpu
from jax.sharding import PartitionSpec as P

HEAD_DIM = 64
EPSILON = 1e-05
VMEM_GRANT = 65280 * 1024
MESH = pl.DeviceIdType.MESH
F32, BF16 = jnp.float32, jnp.bfloat16


def dot(a, b):
    return jnp.dot(a, b, preferred_element_type=F32)


def dot_nt(a, b):
    return lax.dot_general(a, b, (((1,), (1,)), ((), ())), preferred_element_type=F32)


def dot_tn(a, b):
    return lax.dot_general(a, b, (((0,), (0,)), ((), ())), preferred_element_type=F32)


def repeat(count, body, carry):
    if count == 1:
        return body(0, carry)
    return lax.fori_loop(0, count, body, carry)


def kernel(
    n, reduce_here, key_chunk,
    series, target, w_embed, w_query, w_key, w_value, w_out, norm_gain, w_head,
    pred_out, query_out, final_out, gain_out, head_out,
    pack, got, wq, wk, wv, wo, wh, tg, hid, keys, values, powers, pred_half, pred_got,
    no2, gh_all, gh2, gm2, cl_all, cl2, gq_src, gq_all, gains, gain_mine,
    head_src, head_slots, head_full, out_src, out_slots, out_full,
    pair_send, pair_recv, hid_send, hid_recv, gq_send, gq_recv, gain_send, gain_recv,
    hr_send, hr_recv, ha_send, ha_recv, or_send, or_recv, oa_send, oa_recv,
    inputs, embed, head_term_f, head_near, head_sum, out_term_f, out_near, out_sum, gain_row, load_sem,
):
    me = lax.axis_index("var")
    t = lax.axis_index("tm")
    other = 1 - t
    my_id = me * 2 + t
    rows = series.shape[1]
    steps = series.shape[2]
    horizon = 2 * target.shape[2]
    samples = series.shape[0]
    heads_half = w_query.shape[1] // HEAD_DIM
    heads = 2 * heads_half
    block = pl.ds(pl.multiple_of(me * rows, rows), rows)

    def to_pair(index, src, dst):
        return pltpu.make_async_remote_copy(
            src_ref=src, dst_ref=dst, send_sem=pair_send.at[index], recv_sem=pair_recv.at[index],
            device_id={"var": me, "tm": other}, device_id_type=MESH,
        )

    lo, hi, n_hi = lax.rem(me, 2), me // 2, n // 2
    near = hi * 2 + 1 - lo

    def loop(count, body):
        def go(i, carry):
            body(i)
            return carry
        lax.fori_loop(0, count, go, 0)

    def line_peer(i):
        return lax.rem(hi + 1 + i, n_hi)

    def var_copy(peer, src, dst, send_sem, recv_sem):
        return pltpu.make_async_remote_copy(
            src_ref=src, dst_ref=dst, send_sem=send_sem, recv_sem=recv_sem,
            device_id={"var": peer, "tm": t}, device_id_type=MESH,
        )

    def spread(at, send, recv):
        var_copy(near, at(me), at(me), send.at[near], recv.at[me]).start()

        def go(i):
            peer = line_peer(i) * 2 + lo
            var_copy(peer, at(me), at(me), send.at[peer], recv.at[me]).start()
        loop(n_hi - 1, go)

    def forward_blocks(at, send, recv):
        def go(i):
            peer = lax.rem(hi + n_hi - 1 - i, n_hi) * 2 + lo
            var_copy(peer, at(me), at(peer), send.at[peer], recv.at[peer]).wait_recv()
            var_copy(near, at(peer), at(peer), send.at[peer + 1 - 2 * lo], recv.at[peer]).start()
        loop(n_hi - 1, go)

    def settle(at, send, recv, which):
        if which == "recv":
            def go(i):
                block_of = i * 2 + 1 - lo
                var_copy(near, at(me), at(block_of), send.at[near], recv.at[block_of]).wait_recv()
            loop(n_hi, go)
        else:
            def go(i):
                peer = lax.rem(me + 1 + i, n)
                var_copy(near, at(me), at(me), send.at[peer], recv.at[me]).wait_send()
            loop(n - 1, go)

    def near_copy(bf_ref, got_ref, send, recv):
        return var_copy(near, bf_ref.at[1 - lo], got_ref, send.at[near], recv.at[hi * 2])

    def line_sum(term_ref, got_ref, sum_ref, slots, send, recv):
        sum_ref[...] = (term_ref[lo] + got_ref[...].astype(F32)).astype(BF16)

        def go(i):
            peer = line_peer(i)
            at = peer * 2 + lo
            var_copy(at, sum_ref.at[peer], slots.at[hi], send.at[at], recv.at[me]).start()
        loop(n_hi - 1, go)
        slots[hi] = sum_ref[hi]

    def line_wait(sum_ref, slots, send, recv, which):
        def go(i):
            peer = line_peer(i)
            at = peer * 2 + lo
            copy = var_copy(at, sum_ref.at[peer], slots.at[peer], send.at[at], recv.at[at])
            if which == "recv":
                copy.wait_recv()
            else:
                copy.wait_send()
        loop(n_hi - 1, go)

    def everyone(body):
        def go(i, carry):
            where = lax.rem(my_id + 1 + i, 2 * n)
            body(where, where // 2, lax.rem(where, 2))
            return carry
        lax.fori_loop(0, 2 * n - 1, go, 0)

    barrier = pltpu.get_barrier_semaphore()

    def greet(where, p, q):
        pl.semaphore_signal(barrier, inc=1, device_id={"var": p, "tm": q}, device_id_type=MESH)
    everyone(greet)

    pieces = 4
    piece = steps // pieces
    load_series = [pltpu.make_async_copy(series.at[k], inputs.at[k], load_sem.at[k]) for k in range(samples)]
    load_embed = [
        pltpu.make_async_copy(
            w_embed.at[pl.ds(k * piece, piece), :], embed.at[pl.ds(k * piece, piece), :],
            load_sem.at[samples + k],
        )
        for k in range(pieces)
    ]
    base = samples + pieces
    load_rest = [
        pltpu.make_async_copy(src, dst, load_sem.at[base + k])
        for k, (src, dst) in enumerate([
            (w_query, wq.at[t]), (w_key, wk.at[t]), (w_value, wv.at[t]), (w_out, wo.at[t]),
            (w_head, wh.at[t]), (target.at[t], tg.at[t]), (norm_gain, gain_row),
        ])
    ]
    for copy in load_series + load_embed + load_rest:
        copy.start()

    width = w_embed.shape[1]
    shifts = []
    for s in range(samples):
        load_series[s].wait()
        x = inputs[s].astype(F32)
        mean = jnp.mean(x, axis=1, keepdims=True)
        centred = x - mean
        spread_sum = jnp.sum(centred * centred, axis=1, keepdims=True)
        pack[s, :rows, width:width + 128] = jnp.broadcast_to(mean, (rows, 128))
        pack[s, :rows, width + 128:] = jnp.broadcast_to(spread_sum, (rows, 128))
        pack[s, rows:, width:] = jnp.zeros((8, 256), F32)
        shifts.append(centred.astype(BF16))
    shifts.append(jnp.ones((16, steps), BF16))
    left = jnp.concatenate(shifts, axis=0)
    total = None
    for k in range(pieces):
        load_embed[k].wait()
        cols = slice(k * piece, (k + 1) * piece)
        part = dot(left[:, cols], embed[cols, :])
        total = part if total is None else total + part
    for s in range(samples):
        pack[s, :rows, :width] = total[s * rows:(s + 1) * rows]
        pack[s, rows:, :width] = total[samples * rows:samples * rows + 8]

    pl.semaphore_wait(barrier, 2 * n - 1)
    first = to_pair(0, pack.at[other], got)
    first.start()
    weight_copies = [
        to_pair(1, w_query, wq.at[t]),
        to_pair(2, w_key, wk.at[t]),
        to_pair(3, w_value, wv.at[t]),
        to_pair(4, w_out, wo.at[t]),
        to_pair(5, w_head, wh.at[t]),
        to_pair(6, target.at[other], tg.at[t]),
    ]
    for copy in weight_copies:
        copy.start()
    first.wait()

    mean_a, mean_b = pack[t, :rows, width:width + 1], got[:rows, width:width + 1]
    sq_a, sq_b = pack[t, :rows, width + 128:width + 129], got[:rows, width + 128:width + 129]
    center = (mean_a + mean_b) * 0.5
    half_gap = (mean_a - mean_b) * 0.5
    deviation = jnp.sqrt((sq_a + sq_b) * (1.0 / (2 * steps)) + half_gap * half_gap + EPSILON)
    sums_a, sums_b = pack[t, rows:rows + 1, :width], got[rows:rows + 1, :width]
    hidden = (
        (pack[t, :rows, :width] + got[:rows, :width] + half_gap * (sums_a - sums_b)) / deviation
    ).astype(BF16)
    hid[t, block, :] = hidden

    hid_from = lambda p: hid.at[t, pl.ds(pl.multiple_of(p * rows, rows), rows), :]
    spread(hid_from, hid_send, hid_recv)

    for copy in weight_copies + load_rest:
        copy.wait()
    queries = jnp.concatenate([dot(hidden, wq[0]), dot(hidden, wq[1])], axis=1).astype(BF16)
    queries = (queries.astype(F32) * HEAD_DIM ** (-0.5)).astype(BF16)
    q_heads = [queries[:, h * HEAD_DIM:(h + 1) * HEAD_DIM] for h in range(heads)]

    forward_blocks(hid_from, hid_send, hid_recv)
    settle(hid_from, hid_send, hid_recv, "recv")
    relay = to_pair(7, hid.at[t], hid.at[t])
    relay.start()

    chunks = n * rows // key_chunk

    def chunk_rows(c):
        if chunks == 1:
            return pl.ds(0, key_chunk)
        return pl.ds(pl.multiple_of(c * key_chunk, key_chunk), key_chunk)

    def forward(c, carry):
        totals, summed = carry
        at = chunk_rows(c)
        h_rows = hid[t, at, :]
        key_rows = jnp.concatenate([dot(h_rows, wk[0]), dot(h_rows, wk[1])], axis=1).astype(BF16)
        value_rows = jnp.concatenate([dot(h_rows, wv[0]), dot(h_rows, wv[1])], axis=1).astype(BF16)
        keys[at, :] = key_rows
        values[at, :] = value_rows
        new_totals, new_summed = [], []
        for h in range(heads):
            cols = slice(h * HEAD_DIM, (h + 1) * HEAD_DIM)
            p = jnp.exp(dot_nt(q_heads[h], key_rows[:, cols]))
            powers[h, c] = p
            new_totals.append(totals[h] + jnp.sum(p, axis=1, keepdims=True))
            new_summed.append(summed[h] + dot(p.astype(BF16), value_rows[:, cols]))
        return tuple(new_totals), tuple(new_summed)

    zero = (
        tuple(jnp.zeros((rows, 1), F32) for _ in range(heads)),
        tuple(jnp.zeros((rows, HEAD_DIM), F32) for _ in range(heads)),
    )
    totals, summed = repeat(chunks, forward, zero)
    context = jnp.concatenate([summed[h] / totals[h] for h in range(heads)], axis=1)
    context_low = context.astype(BF16)
    half = context.shape[1] // 2
    w_out_all = wo[...].reshape(2 * half, width)
    residual = hidden.astype(F32) + dot(context_low, w_out_all)
    shifted = residual - jnp.mean(residual, axis=1, keepdims=True)
    norm_root = jnp.sqrt(jnp.mean(shifted * shifted, axis=1, keepdims=True) + EPSILON)
    unit_rows = shifted / norm_root
    gain = gain_row[...]
    normal_out = (unit_rows * gain).astype(BF16)
    no2[t] = normal_out
    send_no = to_pair(8, no2.at[t], no2.at[t])
    send_no.start()
    grad_normal = jnp.zeros((rows, width), F32)
    for h in range(2):
        horizon_norm = dot(normal_out, wh[h])
        pred_half[h] = horizon_norm * deviation + center
        errors = horizon_norm - (tg[h] - center) / deviation
        grad_h = (errors * (2.0 / (samples * horizon))).astype(BF16)
        gh_all[h] = grad_h
        grad_normal += dot_nt(grad_h, wh[h])
    send_gh = to_pair(9, gh_all.at[other], gh2.at[t])
    send_gh.start()
    send_pred = to_pair(10, pred_half.at[other], pred_got)
    send_pred.start()
    gh2[t] = gh_all[t]
    pred_out[t] = pred_half[t]

    gain_mine[...] = jnp.sum(grad_normal * unit_rows, axis=0, keepdims=True)
    grad_unit = grad_normal * gain
    grad_mix = (
        (
            grad_unit
            - jnp.mean(grad_unit, axis=1, keepdims=True)
            - unit_rows * jnp.mean(grad_unit * unit_rows, axis=1, keepdims=True)
        )
        / norm_root
    ).astype(BF16)
    gm2[t] = grad_mix
    for h in range(2):
        cl_all[h] = context_low[:, h * half:(h + 1) * half]
    send_gm = to_pair(11, gm2.at[t], gm2.at[t])
    send_gm.start()
    send_cl = to_pair(12, cl_all.at[other], cl2.at[t])
    send_cl.start()
    cl2[t] = cl_all[t]

    def gain_copy(where, p, q, slot):
        return pltpu.make_async_remote_copy(
            src_ref=gain_mine, dst_ref=gains.at[slot], send_sem=gain_send.at[where], recv_sem=gain_recv.at[slot],
            device_id={"var": p, "tm": q}, device_id_type=MESH,
        )

    if reduce_here:
        gains[my_id] = gain_mine[...]
        everyone(lambda where, p, q: gain_copy(where, p, q, my_id).start())
    else:
        gain_out[...] = gain_mine[...]

    send_no.wait()
    send_gh.wait()
    head_term = dot_tn(no2[...].reshape(samples * rows, width), gh2[...].reshape(samples * rows, horizon // 2))
    if reduce_here:
        by_lo = head_term.reshape(n_hi, 2, width // n, horizon // 2)
        for k in range(2):
            head_term_f[k] = by_lo[:, k]
            head_src[k] = by_lo[:, k].astype(BF16)
        head_first = near_copy(head_src, head_near, hr_send, hr_recv)
        head_first.start()
    else:
        head_out[...] = head_term
    grad_context = dot_nt(grad_mix, w_out_all)
    gc_heads, row_dots, scales = [], [], []
    for h in range(heads):
        cols = slice(h * HEAD_DIM, (h + 1) * HEAD_DIM)
        gc_heads.append(grad_context[:, cols].astype(BF16))
        row_dots.append(jnp.sum(grad_context[:, cols] * context[:, cols], axis=1, keepdims=True))
        scales.append(1.0 / totals[h])

    def backward(c, carry):
        at = chunk_rows(c)
        key_rows, value_rows = keys[at, :], values[at, :]
        results = []
        for h in range(heads):
            cols = slice(h * HEAD_DIM, (h + 1) * HEAD_DIM)
            grad_weights = dot_nt(gc_heads[h], value_rows[:, cols])
            grad_scores = (powers[h, c] * scales[h] * (grad_weights - row_dots[h])).astype(BF16)
            results.append(carry[h] + dot(grad_scores, key_rows[:, cols]))
        return tuple(results)

    grads = repeat(chunks, backward, zero[1])
    grad_query = (jnp.concatenate(grads, axis=1) * HEAD_DIM ** (-0.5)).astype(BF16)
    for h in range(2):
        gq_src[h] = grad_query[:, h * half:(h + 1) * half]

    swap = to_pair(13, gq_src.at[other], gq_all.at[t, block, :])
    swap.start()
    gq_all[t, block, :] = gq_src[t]
    gq_from = lambda p: gq_all.at[:, pl.ds(pl.multiple_of(p * rows, rows), rows), :]

    if reduce_here:
        head_first.wait()
        line_sum(head_term_f, head_near, head_sum, head_slots, hr_send, hr_recv)
    send_gm.wait()
    send_cl.wait()
    out_term = dot_tn(cl2[...].reshape(samples * rows, half), gm2[...].reshape(samples * rows, width))
    swap.wait()
    spread(gq_from, gq_send, gq_recv)
    if reduce_here:
        by_lo = out_term.reshape(n_hi, 2, half // n, width)
        for k in range(2):
            out_term_f[k] = by_lo[:, k]
            out_src[k] = by_lo[:, k].astype(BF16)
        out_first = near_copy(out_src, out_near, or_send, or_recv)
        out_first.start()
    else:
        final_out[...] = out_term
    send_pred.wait()
    pred_out[other] = pred_got[...]
    relay.wait()
    forward_blocks(gq_from, gq_send, gq_recv)
    head_from = lambda p: head_full.at[p]
    out_from = lambda p: out_full.at[p]

    if reduce_here:
        out_first.wait()
        line_sum(out_term_f, out_near, out_sum, out_slots, or_send, or_recv)
        line_wait(head_sum, head_slots, hr_send, hr_recv, "recv")
        head_full[me] = jnp.sum(head_slots[...].astype(F32), axis=0).astype(BF16)
        spread(head_from, ha_send, ha_recv)
        line_wait(out_sum, out_slots, or_send, or_recv, "recv")
        out_full[me] = jnp.sum(out_slots[...].astype(F32), axis=0).astype(BF16)
        spread(out_from, oa_send, oa_recv)

    settle(gq_from, gq_send, gq_recv, "recv")
    query_out[...] = dot_tn(
        hid[...].reshape(samples * n * rows, width), gq_all[...].reshape(samples * n * rows, half)
    )
    if reduce_here:
        forward_blocks(head_from, ha_send, ha_recv)
        forward_blocks(out_from, oa_send, oa_recv)
        everyone(lambda where, p, q: gain_copy(where, p, q, where).wait_recv())
        gain_out[...] = jnp.sum(gains[...], axis=0)
        settle(head_from, ha_send, ha_recv, "recv")
        head_out[...] = head_full[...].reshape(head_out.shape)
        settle(out_from, oa_send, oa_recv, "recv")
        final_out[...] = out_full[...].astype(F32).reshape(final_out.shape)

    settle(hid_from, hid_send, hid_recv, "send")
    settle(gq_from, gq_send, gq_recv, "send")
    if reduce_here:
        everyone(lambda where, p, q: gain_copy(where, p, q, my_id).wait_send())
        line_wait(head_sum, head_slots, hr_send, hr_recv, "send")
        line_wait(out_sum, out_slots, or_send, or_recv, "send")
        settle(head_from, ha_send, ha_recv, "send")
        settle(out_from, oa_send, oa_recv, "send")


def deliver(*refs):
    count = (len(refs) - 1) // 2
    sems = refs[-1]
    copies = [pltpu.make_async_copy(refs[k], refs[count + k], sems.at[k]) for k in range(count)]
    for copy in copies:
        copy.start()
    for copy in copies:
        copy.wait()


def solution(mesh):
    n = mesh.shape["var"]

    def per_device(series, target, w_embed, w_query, w_key, w_value, w_out, norm_gain, w_head):
        samples, rows, steps = series.shape
        width = w_embed.shape[1]
        half = w_query.shape[1]
        hor = target.shape[2]
        heads = 2 * half // HEAD_DIM
        key_chunk = min(512, n * rows)
        chunks = n * rows // key_chunk
        reduce_here = width % (16 * n) == 0 and half % (16 * n) == 0
        cuts = n if reduce_here else 1
        line = n // 2 if reduce_here else 1
        v = pltpu.VMEM
        dma = pltpu.SemaphoreType.DMA
        outs = pl.pallas_call(
            functools.partial(kernel, n, reduce_here, key_chunk),
            out_shape=(
                jax.ShapeDtypeStruct((samples, rows, hor), F32),
                jax.ShapeDtypeStruct((width, half), F32),
                jax.ShapeDtypeStruct((half, width), F32),
                jax.ShapeDtypeStruct((1, width), F32),
                jax.ShapeDtypeStruct((width, hor), BF16 if reduce_here else F32),
            ),
            in_specs=[pl.BlockSpec(memory_space=pltpu.HBM)] * 8 + [pl.BlockSpec(memory_space=pltpu.VMEM)],
            out_specs=[pl.BlockSpec(memory_space=pltpu.VMEM)] * 5,
            scratch_shapes=[
                v((samples, rows + 8, width + 256), F32),
                v((rows + 8, width + 256), F32),
                v((2, width, half), BF16),
                v((2, width, half), BF16),
                v((2, width, half), BF16),
                v((2, half, width), BF16),
                v((2, width, hor), BF16),
                v((2, rows, hor), F32),
                v((samples, n * rows, width), BF16),
                v((n * rows, 2 * half), BF16),
                v((n * rows, 2 * half), BF16),
                v((heads, chunks, rows, key_chunk), F32),
                v((2, rows, hor), F32),
                v((rows, hor), F32),
                v((samples, rows, width), BF16),
                v((2, rows, hor), BF16),
                v((samples, rows, hor), BF16),
                v((samples, rows, width), BF16),
                v((2, rows, half), BF16),
                v((samples, rows, half), BF16),
                v((2, rows, half), BF16),
                v((samples, n * rows, half), BF16),
                v((2 * cuts, 1, width), F32),
                v((1, width), F32),
                v((2, line, width // cuts, hor), BF16),
                v((line, width // cuts, hor), BF16),
                v((cuts, width // cuts, hor), BF16),
                v((2, line, half // cuts, width), BF16),
                v((line, half // cuts, width), BF16),
                v((cuts, half // cuts, width), BF16),
                dma((14,)), dma((14,)),
                dma((n,)), dma((n,)),
                dma((n,)), dma((n,)),
                dma((2 * n,)), dma((2 * n,)),
                dma((n,)), dma((n,)), dma((n,)), dma((n,)),
                dma((n,)), dma((n,)), dma((n,)), dma((n,)),
                v((samples, rows, steps), BF16),
                v((steps, width), BF16),
                v((2, line, width // cuts, hor), F32),
                v((line, width // cuts, hor), BF16),
                v((line, width // cuts, hor), BF16),
                v((2, line, half // cuts, width), F32),
                v((line, half // cuts, width), BF16),
                v((line, half // cuts, width), BF16),
                v((1, width), F32),
                dma((samples + 11,)),
            ],
            compiler_params=pltpu.CompilerParams(
                collective_id=0,
                has_side_effects=True,
                vmem_limit_bytes=VMEM_GRANT,
            ),
        )(series, target, w_embed, w_query, w_key, w_value, w_out, norm_gain.reshape(1, width), w_head)
        pred, query, final, gain, head = outs
        if not reduce_here:
            final, gain, head = lax.psum((final, gain, head), "var")
            gain = lax.psum(gain, "tm")
            return pred, query, final, gain.reshape(width), head
        plain = (pred, query, final, gain)
        pred, query, final, gain = pl.pallas_call(
            deliver,
            out_shape=tuple(jax.ShapeDtypeStruct(x.shape, x.dtype) for x in plain),
            in_specs=[pl.BlockSpec(memory_space=pl.ANY)] * 4,
            out_specs=[pl.BlockSpec(memory_space=pltpu.HBM)] * 4,
            scratch_shapes=[dma((4,))],
        )(*plain)
        return pred, query, final, gain.reshape(width), head.astype(F32)

    in_specs = (
        P("groups", "var", "tm"),
        P("groups", "var", "tm"),
        P("tm", None),
        P(None, "tm"),
        P(None, "tm"),
        P(None, "tm"),
        P("tm", None),
        P(),
        P(None, "tm"),
    )
    out_specs = (
        P("groups", "var", "tm"),
        P("groups", "tm"),
        P(("groups", "tm"), None),
        P("groups"),
        P("groups", "tm"),
    )
    return jax.shard_map(
        per_device, mesh=mesh, in_specs=in_specs, out_specs=out_specs, check_vma=False
    )
```

```python
import functools

import jax
import jax.numpy as jnp
from jax import lax
from jax.experimental import pallas as pl
from jax.experimental.pallas import tpu as pltpu
from jax.sharding import PartitionSpec as P

HEAD_DIM = 64
EPSILON = 1e-05
VMEM_GRANT = 65280 * 1024
MESH = pl.DeviceIdType.MESH
F32, BF16 = jnp.float32, jnp.bfloat16


def dot(a, b):
    return jnp.dot(a, b, preferred_element_type=F32)


def dot_nt(a, b):
    return lax.dot_general(a, b, (((1,), (1,)), ((), ())), preferred_element_type=F32)


def dot_tn(a, b):
    return lax.dot_general(a, b, (((0,), (0,)), ((), ())), preferred_element_type=F32)


def repeat(count, body, carry):
    if count == 1:
        return body(0, carry)
    return lax.fori_loop(0, count, body, carry)


def kernel(
    n, reduce_here, key_chunk,
    series, target, w_embed, w_query, w_key, w_value, w_out, norm_gain, w_head,
    pred_out, query_out, final_out, gain_out, head_out,
    pack, got, wq, wk, wv, wo, wh, tg, hid, keys, values, powers, pred_half, pred_got,
    no2, gh_all, gh2, gm2, cl_all, cl2, gq_src, gq_all, gains, gain_mine,
    head_src, head_slots, head_full, out_src, out_slots, out_full,
    pair_send, pair_recv, hid_send, hid_recv, gq_send, gq_recv, gain_send, gain_recv,
    hr_send, hr_recv, ha_send, ha_recv, or_send, or_recv, oa_send, oa_recv,
    inputs, embed, head_term_f, head_near, head_sum, out_term_f, out_near, out_sum, gain_row, load_sem,
):
    me = lax.axis_index("var")
    t = lax.axis_index("tm")
    other = 1 - t
    my_id = me * 2 + t
    rows = series.shape[1]
    steps = series.shape[2]
    horizon = 2 * target.shape[2]
    samples = series.shape[0]
    heads_half = w_query.shape[1] // HEAD_DIM
    heads = 2 * heads_half
    block = pl.ds(pl.multiple_of(me * rows, rows), rows)

    def to_pair(index, src, dst):
        return pltpu.make_async_remote_copy(
            src_ref=src, dst_ref=dst, send_sem=pair_send.at[index], recv_sem=pair_recv.at[index],
            device_id={"var": me, "tm": other}, device_id_type=MESH,
        )

    lo, hi, n_hi = lax.rem(me, 2), me // 2, n // 2
    near = hi * 2 + 1 - lo

    def loop(count, body):
        def go(i, carry):
            body(i)
            return carry
        lax.fori_loop(0, count, go, 0)

    def line_peer(i):
        return lax.rem(hi + 1 + i, n_hi)

    def var_copy(peer, src, dst, send_sem, recv_sem):
        return pltpu.make_async_remote_copy(
            src_ref=src, dst_ref=dst, send_sem=send_sem, recv_sem=recv_sem,
            device_id={"var": peer, "tm": t}, device_id_type=MESH,
        )

    def spread(at, send, recv):
        var_copy(near, at(me), at(me), send.at[near], recv.at[me]).start()

        def go(i):
            peer = line_peer(i) * 2 + lo
            var_copy(peer, at(me), at(me), send.at[peer], recv.at[me]).start()
        loop(n_hi - 1, go)

    def forward_blocks(at, send, recv):
        def go(i):
            peer = lax.rem(hi + n_hi - 1 - i, n_hi) * 2 + lo
            var_copy(peer, at(me), at(peer), send.at[peer], recv.at[peer]).wait_recv()
            var_copy(near, at(peer), at(peer), send.at[peer + 1 - 2 * lo], recv.at[peer]).start()
        loop(n_hi - 1, go)

    def settle(at, send, recv, which):
        if which == "recv":
            def go(i):
                block_of = i * 2 + 1 - lo
                var_copy(near, at(me), at(block_of), send.at[near], recv.at[block_of]).wait_recv()
            loop(n_hi, go)
        else:
            def go(i):
                peer = lax.rem(me + 1 + i, n)
                var_copy(near, at(me), at(me), send.at[peer], recv.at[me]).wait_send()
            loop(n - 1, go)

    def near_copy(bf_ref, got_ref, send, recv):
        return var_copy(near, bf_ref.at[1 - lo], got_ref, send.at[near], recv.at[hi * 2])

    def line_sum(term_ref, got_ref, sum_ref, slots, send, recv):
        sum_ref[...] = (term_ref[lo] + got_ref[...].astype(F32)).astype(BF16)

        def go(i):
            peer = line_peer(i)
            at = peer * 2 + lo
            var_copy(at, sum_ref.at[peer], slots.at[hi], send.at[at], recv.at[me]).start()
        loop(n_hi - 1, go)
        slots[hi] = sum_ref[hi]

    def line_wait(sum_ref, slots, send, recv, which):
        def go(i):
            peer = line_peer(i)
            at = peer * 2 + lo
            copy = var_copy(at, sum_ref.at[peer], slots.at[peer], send.at[at], recv.at[at])
            if which == "recv":
                copy.wait_recv()
            else:
                copy.wait_send()
        loop(n_hi - 1, go)

    def everyone(body):
        def go(i, carry):
            where = lax.rem(my_id + 1 + i, 2 * n)
            body(where, where // 2, lax.rem(where, 2))
            return carry
        lax.fori_loop(0, 2 * n - 1, go, 0)

    barrier = pltpu.get_barrier_semaphore()

    def greet(where, p, q):
        pl.semaphore_signal(barrier, inc=1, device_id={"var": p, "tm": q}, device_id_type=MESH)
    everyone(greet)

    pieces = 4
    piece = steps // pieces
    load_series = [pltpu.make_async_copy(series.at[k], inputs.at[k], load_sem.at[k]) for k in range(samples)]
    load_embed = [
        pltpu.make_async_copy(
            w_embed.at[pl.ds(k * piece, piece), :], embed.at[pl.ds(k * piece, piece), :],
            load_sem.at[samples + k],
        )
        for k in range(pieces)
    ]
    base = samples + pieces
    load_rest = [
        pltpu.make_async_copy(src, dst, load_sem.at[base + k])
        for k, (src, dst) in enumerate([
            (w_query, wq.at[t]), (w_key, wk.at[t]), (w_value, wv.at[t]), (w_out, wo.at[t]),
            (w_head, wh.at[t]), (target.at[t], tg.at[t]), (norm_gain, gain_row),
        ])
    ]
    for copy in load_series + load_embed + load_rest:
        copy.start()

    width = w_embed.shape[1]
    shifts = []
    for s in range(samples):
        load_series[s].wait()
        x = inputs[s].astype(F32)
        mean = jnp.mean(x, axis=1, keepdims=True)
        centred = x - mean
        spread_sum = jnp.sum(centred * centred, axis=1, keepdims=True)
        pack[s, :rows, width:width + 128] = jnp.broadcast_to(mean, (rows, 128))
        pack[s, :rows, width + 128:] = jnp.broadcast_to(spread_sum, (rows, 128))
        pack[s, rows:, width:] = jnp.zeros((8, 256), F32)
        shifts.append(centred.astype(BF16))
    shifts.append(jnp.ones((16, steps), BF16))
    left = jnp.concatenate(shifts, axis=0)
    total = None
    for k in range(pieces):
        load_embed[k].wait()
        cols = slice(k * piece, (k + 1) * piece)
        part = dot(left[:, cols], embed[cols, :])
        total = part if total is None else total + part
    for s in range(samples):
        pack[s, :rows, :width] = total[s * rows:(s + 1) * rows]
        pack[s, rows:, :width] = total[samples * rows:samples * rows + 8]

    pl.semaphore_wait(barrier, 2 * n - 1)
    first = to_pair(0, pack.at[other], got)
    first.start()
    weight_copies = [
        to_pair(1, w_query, wq.at[t]),
        to_pair(2, w_key, wk.at[t]),
        to_pair(3, w_value, wv.at[t]),
        to_pair(4, w_out, wo.at[t]),
        to_pair(5, w_head, wh.at[t]),
        to_pair(6, target.at[other], tg.at[t]),
    ]
    for copy in weight_copies:
        copy.start()
    first.wait()

    mean_a, mean_b = pack[t, :rows, width:width + 1], got[:rows, width:width + 1]
    sq_a, sq_b = pack[t, :rows, width + 128:width + 129], got[:rows, width + 128:width + 129]
    center = (mean_a + mean_b) * 0.5
    half_gap = (mean_a - mean_b) * 0.5
    deviation = jnp.sqrt((sq_a + sq_b) * (1.0 / (2 * steps)) + half_gap * half_gap + EPSILON)
    sums_a, sums_b = pack[t, rows:rows + 1, :width], got[rows:rows + 1, :width]
    hidden = (
        (pack[t, :rows, :width] + got[:rows, :width] + half_gap * (sums_a - sums_b)) / deviation
    ).astype(BF16)
    hid[t, block, :] = hidden

    hid_from = lambda p: hid.at[t, pl.ds(pl.multiple_of(p * rows, rows), rows), :]
    spread(hid_from, hid_send, hid_recv)

    for copy in weight_copies + load_rest:
        copy.wait()
    queries = jnp.concatenate([dot(hidden, wq[0]), dot(hidden, wq[1])], axis=1).astype(BF16)
    queries = (queries.astype(F32) * HEAD_DIM ** (-0.5)).astype(BF16)
    q_heads = [queries[:, h * HEAD_DIM:(h + 1) * HEAD_DIM] for h in range(heads)]

    forward_blocks(hid_from, hid_send, hid_recv)
    settle(hid_from, hid_send, hid_recv, "recv")
    relay = to_pair(7, hid.at[t], hid.at[t])
    relay.start()

    chunks = n * rows // key_chunk

    def chunk_rows(c):
        if chunks == 1:
            return pl.ds(0, key_chunk)
        return pl.ds(pl.multiple_of(c * key_chunk, key_chunk), key_chunk)

    def forward(c, carry):
        totals, summed = carry
        at = chunk_rows(c)
        h_rows = hid[t, at, :]
        key_rows = jnp.concatenate([dot(h_rows, wk[0]), dot(h_rows, wk[1])], axis=1).astype(BF16)
        value_rows = jnp.concatenate([dot(h_rows, wv[0]), dot(h_rows, wv[1])], axis=1).astype(BF16)
        keys[at, :] = key_rows
        values[at, :] = value_rows
        new_totals, new_summed = [], []
        for h in range(heads):
            cols = slice(h * HEAD_DIM, (h + 1) * HEAD_DIM)
            p = jnp.exp(dot_nt(q_heads[h], key_rows[:, cols]))
            powers[h, c] = p
            new_totals.append(totals[h] + jnp.sum(p, axis=1, keepdims=True))
            new_summed.append(summed[h] + dot(p.astype(BF16), value_rows[:, cols]))
        return tuple(new_totals), tuple(new_summed)

    zero = (
        tuple(jnp.zeros((rows, 1), F32) for _ in range(heads)),
        tuple(jnp.zeros((rows, HEAD_DIM), F32) for _ in range(heads)),
    )
    totals, summed = repeat(chunks, forward, zero)
    context = jnp.concatenate([summed[h] / totals[h] for h in range(heads)], axis=1)
    context_low = context.astype(BF16)
    half = context.shape[1] // 2
    w_out_all = wo[...].reshape(2 * half, width)
    residual = hidden.astype(F32) + dot(context_low, w_out_all)
    shifted = residual - jnp.mean(residual, axis=1, keepdims=True)
    norm_root = jnp.sqrt(jnp.mean(shifted * shifted, axis=1, keepdims=True) + EPSILON)
    unit_rows = shifted / norm_root
    gain = gain_row[...]
    normal_out = (unit_rows * gain).astype(BF16)
    no2[t] = normal_out
    send_no = to_pair(8, no2.at[t], no2.at[t])
    send_no.start()
    grad_normal = jnp.zeros((rows, width), F32)
    for h in range(2):
        horizon_norm = dot(normal_out, wh[h])
        pred_half[h] = horizon_norm * deviation + center
        errors = horizon_norm - (tg[h] - center) / deviation
        grad_h = (errors * (2.0 / (samples * horizon))).astype(BF16)
        gh_all[h] = grad_h
        grad_normal += dot_nt(grad_h, wh[h])
    send_gh = to_pair(9, gh_all.at[other], gh2.at[t])
    send_gh.start()
    send_pred = to_pair(10, pred_half.at[other], pred_got)
    send_pred.start()
    gh2[t] = gh_all[t]
    pred_out[t] = pred_half[t]

    gain_mine[...] = jnp.sum(grad_normal * unit_rows, axis=0, keepdims=True)
    grad_unit = grad_normal * gain
    grad_mix = (
        (
            grad_unit
            - jnp.mean(grad_unit, axis=1, keepdims=True)
            - unit_rows * jnp.mean(grad_unit * unit_rows, axis=1, keepdims=True)
        )
        / norm_root
    ).astype(BF16)
    gm2[t] = grad_mix
    for h in range(2):
        cl_all[h] = context_low[:, h * half:(h + 1) * half]
    send_gm = to_pair(11, gm2.at[t], gm2.at[t])
    send_gm.start()
    send_cl = to_pair(12, cl_all.at[other], cl2.at[t])
    send_cl.start()
    cl2[t] = cl_all[t]

    def gain_copy(where, p, q, slot):
        return pltpu.make_async_remote_copy(
            src_ref=gain_mine, dst_ref=gains.at[slot], send_sem=gain_send.at[where], recv_sem=gain_recv.at[slot],
            device_id={"var": p, "tm": q}, device_id_type=MESH,
        )

    if reduce_here:
        gains[my_id] = gain_mine[...]
        everyone(lambda where, p, q: gain_copy(where, p, q, my_id).start())
    else:
        gain_out[...] = gain_mine[...]

    send_no.wait()
    send_gh.wait()
    head_term = dot_tn(no2[...].reshape(samples * rows, width), gh2[...].reshape(samples * rows, horizon // 2))
    if reduce_here:
        by_lo = head_term.reshape(n_hi, 2, width // n, horizon // 2)
        for k in range(2):
            head_term_f[k] = by_lo[:, k]
            head_src[k] = by_lo[:, k].astype(BF16)
        head_first = near_copy(head_src, head_near, hr_send, hr_recv)
        head_first.start()
    else:
        head_out[...] = head_term
    grad_context = dot_nt(grad_mix, w_out_all)
    gc_heads, row_dots, scales = [], [], []
    for h in range(heads):
        cols = slice(h * HEAD_DIM, (h + 1) * HEAD_DIM)
        gc_heads.append(grad_context[:, cols].astype(BF16))
        row_dots.append(jnp.sum(grad_context[:, cols] * context[:, cols], axis=1, keepdims=True))
        scales.append(1.0 / totals[h])

    def backward(c, carry):
        at = chunk_rows(c)
        key_rows, value_rows = keys[at, :], values[at, :]
        results = []
        for h in range(heads):
            cols = slice(h * HEAD_DIM, (h + 1) * HEAD_DIM)
            grad_weights = dot_nt(gc_heads[h], value_rows[:, cols])
            grad_scores = (powers[h, c] * scales[h] * (grad_weights - row_dots[h])).astype(BF16)
            results.append(carry[h] + dot(grad_scores, key_rows[:, cols]))
        return tuple(results)

    grads = repeat(chunks, backward, zero[1])
    grad_query = (jnp.concatenate(grads, axis=1) * HEAD_DIM ** (-0.5)).astype(BF16)
    for h in range(2):
        gq_src[h] = grad_query[:, h * half:(h + 1) * half]

    swap = to_pair(13, gq_src.at[other], gq_all.at[t, block, :])
    swap.start()
    gq_all[t, block, :] = gq_src[t]
    gq_from = lambda p: gq_all.at[:, pl.ds(pl.multiple_of(p * rows, rows), rows), :]

    if reduce_here:
        head_first.wait()
        line_sum(head_term_f, head_near, head_sum, head_slots, hr_send, hr_recv)
    send_gm.wait()
    send_cl.wait()
    out_term = dot_tn(cl2[...].reshape(samples * rows, half), gm2[...].reshape(samples * rows, width))
    swap.wait()
    spread(gq_from, gq_send, gq_recv)
    if reduce_here:
        by_lo = out_term.reshape(n_hi, 2, half // n, width)
        for k in range(2):
            out_term_f[k] = by_lo[:, k]
            out_src[k] = by_lo[:, k].astype(BF16)
        out_first = near_copy(out_src, out_near, or_send, or_recv)
        out_first.start()
    else:
        final_out[...] = out_term
    send_pred.wait()
    pred_out[other] = pred_got[...]
    relay.wait()
    forward_blocks(gq_from, gq_send, gq_recv)
    head_from = lambda p: head_full.at[p]
    out_from = lambda p: out_full.at[p]

    if reduce_here:
        out_first.wait()
        line_sum(out_term_f, out_near, out_sum, out_slots, or_send, or_recv)
        line_wait(head_sum, head_slots, hr_send, hr_recv, "recv")
        head_full[me] = jnp.sum(head_slots[...].astype(F32), axis=0).astype(BF16)
        spread(head_from, ha_send, ha_recv)
        line_wait(out_sum, out_slots, or_send, or_recv, "recv")
        out_full[me] = jnp.sum(out_slots[...].astype(F32), axis=0).astype(BF16)
        spread(out_from, oa_send, oa_recv)

    settle(gq_from, gq_send, gq_recv, "recv")
    query_out[...] = dot_tn(
        gq_all[...].reshape(samples * n * rows, half), hid[...].reshape(samples * n * rows, width)
    ).T
    if reduce_here:
        forward_blocks(head_from, ha_send, ha_recv)
        forward_blocks(out_from, oa_send, oa_recv)
        everyone(lambda where, p, q: gain_copy(where, p, q, where).wait_recv())
        gain_out[...] = jnp.sum(gains[...], axis=0)
        settle(head_from, ha_send, ha_recv, "recv")
        head_out[...] = head_full[...].reshape(head_out.shape)
        settle(out_from, oa_send, oa_recv, "recv")
        final_out[...] = out_full[...].astype(F32).reshape(final_out.shape)

    settle(hid_from, hid_send, hid_recv, "send")
    settle(gq_from, gq_send, gq_recv, "send")
    if reduce_here:
        everyone(lambda where, p, q: gain_copy(where, p, q, my_id).wait_send())
        line_wait(head_sum, head_slots, hr_send, hr_recv, "send")
        line_wait(out_sum, out_slots, or_send, or_recv, "send")
        settle(head_from, ha_send, ha_recv, "send")
        settle(out_from, oa_send, oa_recv, "send")


def deliver(*refs):
    count = (len(refs) - 4) // 3
    sources, results, held = refs[:count], refs[count:2 * count], refs[2 * count:3 * count]
    turned, in_sems, out_sems, turned_sem = refs[3 * count:]
    arrive = [pltpu.make_async_copy(sources[k], held[k], in_sems.at[k]) for k in range(count)]
    leave = [pltpu.make_async_copy(held[k], results[k], out_sems.at[k]) for k in range(count - 1)]
    for copy in arrive:
        copy.start()
    for k in range(count - 1):
        arrive[k].wait()
        leave[k].start()
    arrive[count - 1].wait()
    turned[...] = held[count - 1][...].astype(F32).T
    last = pltpu.make_async_copy(turned, results[count - 1], turned_sem)
    last.start()
    for copy in leave + [last]:
        copy.wait()


def solution(mesh):
    n = mesh.shape["var"]

    def per_device(series, target, w_embed, w_query, w_key, w_value, w_out, norm_gain, w_head):
        samples, rows, steps = series.shape
        width = w_embed.shape[1]
        half = w_query.shape[1]
        hor = target.shape[2]
        heads = 2 * half // HEAD_DIM
        key_chunk = min(512, n * rows)
        chunks = n * rows // key_chunk
        reduce_here = width % (16 * n) == 0 and half % (16 * n) == 0
        cuts = n if reduce_here else 1
        line = n // 2 if reduce_here else 1
        v = pltpu.VMEM
        dma = pltpu.SemaphoreType.DMA
        outs = pl.pallas_call(
            functools.partial(kernel, n, reduce_here, key_chunk),
            out_shape=(
                jax.ShapeDtypeStruct((samples, rows, hor), F32),
                jax.ShapeDtypeStruct((width, half), F32),
                jax.ShapeDtypeStruct((half, width), F32),
                jax.ShapeDtypeStruct((1, width), F32),
                jax.ShapeDtypeStruct((width, hor), BF16 if reduce_here else F32),
            ),
            in_specs=[pl.BlockSpec(memory_space=pltpu.HBM)] * 8 + [pl.BlockSpec(memory_space=pltpu.VMEM)],
            out_specs=[pl.BlockSpec(memory_space=pltpu.VMEM)] * 5,
            scratch_shapes=[
                v((samples, rows + 8, width + 256), F32),
                v((rows + 8, width + 256), F32),
                v((2, width, half), BF16),
                v((2, width, half), BF16),
                v((2, width, half), BF16),
                v((2, half, width), BF16),
                v((2, width, hor), BF16),
                v((2, rows, hor), F32),
                v((samples, n * rows, width), BF16),
                v((n * rows, 2 * half), BF16),
                v((n * rows, 2 * half), BF16),
                v((heads, chunks, rows, key_chunk), F32),
                v((2, rows, hor), F32),
                v((rows, hor), F32),
                v((samples, rows, width), BF16),
                v((2, rows, hor), BF16),
                v((samples, rows, hor), BF16),
                v((samples, rows, width), BF16),
                v((2, rows, half), BF16),
                v((samples, rows, half), BF16),
                v((2, rows, half), BF16),
                v((samples, n * rows, half), BF16),
                v((2 * cuts, 1, width), F32),
                v((1, width), F32),
                v((2, line, width // cuts, hor), BF16),
                v((line, width // cuts, hor), BF16),
                v((cuts, width // cuts, hor), BF16),
                v((2, line, half // cuts, width), BF16),
                v((line, half // cuts, width), BF16),
                v((cuts, half // cuts, width), BF16),
                dma((14,)), dma((14,)),
                dma((n,)), dma((n,)),
                dma((n,)), dma((n,)),
                dma((2 * n,)), dma((2 * n,)),
                dma((n,)), dma((n,)), dma((n,)), dma((n,)),
                dma((n,)), dma((n,)), dma((n,)), dma((n,)),
                v((samples, rows, steps), BF16),
                v((steps, width), BF16),
                v((2, line, width // cuts, hor), F32),
                v((line, width // cuts, hor), BF16),
                v((line, width // cuts, hor), BF16),
                v((2, line, half // cuts, width), F32),
                v((line, half // cuts, width), BF16),
                v((line, half // cuts, width), BF16),
                v((1, width), F32),
                dma((samples + 11,)),
            ],
            compiler_params=pltpu.CompilerParams(
                collective_id=0,
                has_side_effects=True,
                vmem_limit_bytes=VMEM_GRANT,
            ),
        )(series, target, w_embed, w_query, w_key, w_value, w_out, norm_gain.reshape(1, width), w_head)
        pred, query, final, gain, head = outs
        if not reduce_here:
            final, gain, head = lax.psum((final, gain, head), "var")
            gain = lax.psum(gain, "tm")
            return pred, query, final, gain.reshape(width), head
        plain = (pred, query, final, gain, head)
        shapes = [jax.ShapeDtypeStruct(x.shape, x.dtype) for x in plain[:4]]
        shapes.append(jax.ShapeDtypeStruct((hor, width), F32))
        pred, query, final, gain, head = pl.pallas_call(
            deliver,
            out_shape=tuple(shapes),
            in_specs=[pl.BlockSpec(memory_space=pltpu.HBM)] * 5,
            out_specs=[pl.BlockSpec(memory_space=pltpu.HBM)] * 5,
            scratch_shapes=[v(x.shape, x.dtype) for x in plain]
            + [v((hor, width), F32), dma((5,)), dma((4,)), dma(())],
            compiler_params=pltpu.CompilerParams(vmem_limit_bytes=VMEM_GRANT),
        )(*plain)
        return pred, query, final, gain.reshape(width), jnp.transpose(head)

    in_specs = (
        P("groups", "var", "tm"),
        P("groups", "var", "tm"),
        P("tm", None),
        P(None, "tm"),
        P(None, "tm"),
        P(None, "tm"),
        P("tm", None),
        P(),
        P(None, "tm"),
    )
    out_specs = (
        P("groups", "var", "tm"),
        P("groups", "tm"),
        P(("groups", "tm"), None),
        P("groups"),
        P("groups", "tm"),
    )
    return jax.shard_map(
        per_device, mesh=mesh, in_specs=in_specs, out_specs=out_specs, check_vma=False
    )
```

```python
import functools

import jax
import jax.numpy as jnp
from jax import lax
from jax.experimental import pallas as pl
from jax.experimental.pallas import tpu as pltpu
from jax.sharding import PartitionSpec as P

HEAD_DIM = 64
EPSILON = 1e-05
VMEM_GRANT = 65280 * 1024
MESH = pl.DeviceIdType.MESH
F32, BF16 = jnp.float32, jnp.bfloat16


def dot(a, b):
    return jnp.dot(a, b, preferred_element_type=F32)


def dot_nt(a, b):
    return lax.dot_general(a, b, (((1,), (1,)), ((), ())), preferred_element_type=F32)


def dot_tn(a, b):
    return lax.dot_general(a, b, (((0,), (0,)), ((), ())), preferred_element_type=F32)


def repeat(count, body, carry):
    if count == 1:
        return body(0, carry)
    return lax.fori_loop(0, count, body, carry)


def kernel(
    n, reduce_here, key_chunk,
    series, target, w_embed, w_query, w_key, w_value, w_out, norm_gain, w_head,
    pred_out, query_out, final_out, gain_out, head_out,
    pack, got, wq, wk, wv, wo, wh, tg, hid, keys, values, powers, pred_half, pred_got,
    no2, gh_all, gh2, gm2, cl_all, cl2, gq_src, gq_all, gains, gain_mine,
    head_src, head_slots, head_full, out_src, out_slots, out_full,
    pair_send, pair_recv, hid_send, hid_recv, gq_send, gq_recv, gain_send, gain_recv,
    hr_send, hr_recv, ha_send, ha_recv, or_send, or_recv, oa_send, oa_recv,
    inputs, embed, head_term_f, head_near, head_sum, out_term_f, out_near, out_sum, gain_row, load_sem,
):
    me = lax.axis_index("var")
    t = lax.axis_index("tm")
    other = 1 - t
    my_id = me * 2 + t
    rows = series.shape[1]
    steps = series.shape[2]
    horizon = 2 * target.shape[2]
    samples = series.shape[0]
    heads_half = w_query.shape[1] // HEAD_DIM
    heads = 2 * heads_half
    block = pl.ds(pl.multiple_of(me * rows, rows), rows)

    def to_pair(index, src, dst):
        return pltpu.make_async_remote_copy(
            src_ref=src, dst_ref=dst, send_sem=pair_send.at[index], recv_sem=pair_recv.at[index],
            device_id={"var": me, "tm": other}, device_id_type=MESH,
        )

    lo, hi, n_hi = lax.rem(me, 2), me // 2, n // 2
    near = hi * 2 + 1 - lo

    def loop(count, body):
        def go(i, carry):
            body(i)
            return carry
        lax.fori_loop(0, count, go, 0)

    def line_peer(i):
        upper = 2 * hi // n_hi
        place = hi + upper * (n_hi - 1 - 2 * hi)
        beyond = (i + n_hi - 2 * place) // n_hi
        beside = place + (i // 2 + 1) * (1 - 2 * (i % 2))
        peer = beyond * (i + 1) + (1 - beyond) * beside
        return peer + upper * (n_hi - 1 - 2 * peer)

    def var_copy(peer, src, dst, send_sem, recv_sem):
        return pltpu.make_async_remote_copy(
            src_ref=src, dst_ref=dst, send_sem=send_sem, recv_sem=recv_sem,
            device_id={"var": peer, "tm": t}, device_id_type=MESH,
        )

    def spread(at, send, recv):
        var_copy(near, at(me), at(me), send.at[near], recv.at[me]).start()

        def go(i):
            peer = line_peer(i) * 2 + lo
            var_copy(peer, at(me), at(me), send.at[peer], recv.at[me]).start()
        loop(n_hi - 1, go)

    def forward_blocks(at, send, recv):
        def go(i):
            peer = line_peer(i) * 2 + lo
            var_copy(peer, at(me), at(peer), send.at[peer], recv.at[peer]).wait_recv()
            var_copy(near, at(peer), at(peer), send.at[peer + 1 - 2 * lo], recv.at[peer]).start()
        loop(n_hi - 1, go)

    def settle(at, send, recv, which):
        if which == "recv":
            def go(i):
                block_of = i * 2 + 1 - lo
                var_copy(near, at(me), at(block_of), send.at[near], recv.at[block_of]).wait_recv()
            loop(n_hi, go)
        else:
            def go(i):
                peer = lax.rem(me + 1 + i, n)
                var_copy(near, at(me), at(me), send.at[peer], recv.at[me]).wait_send()
            loop(n - 1, go)

    def near_copy(bf_ref, got_ref, send, recv):
        return var_copy(near, bf_ref.at[1 - lo], got_ref, send.at[near], recv.at[hi * 2])

    def line_sum(term_ref, got_ref, sum_ref, slots, send, recv):
        sum_ref[...] = (term_ref[lo] + got_ref[...].astype(F32)).astype(BF16)

        def go(i):
            peer = line_peer(i)
            at = peer * 2 + lo
            var_copy(at, sum_ref.at[peer], slots.at[hi], send.at[at], recv.at[me]).start()
        loop(n_hi - 1, go)
        slots[hi] = sum_ref[hi]

    def line_wait(sum_ref, slots, send, recv, which):
        def go(i):
            peer = line_peer(i)
            at = peer * 2 + lo
            copy = var_copy(at, sum_ref.at[peer], slots.at[peer], send.at[at], recv.at[at])
            if which == "recv":
                copy.wait_recv()
            else:
                copy.wait_send()
        loop(n_hi - 1, go)

    def everyone(body):
        def go(i, carry):
            where = lax.rem(my_id + 1 + i, 2 * n)
            body(where, where // 2, lax.rem(where, 2))
            return carry
        lax.fori_loop(0, 2 * n - 1, go, 0)

    barrier = pltpu.get_barrier_semaphore()

    def greet(where, p, q):
        pl.semaphore_signal(barrier, inc=1, device_id={"var": p, "tm": q}, device_id_type=MESH)
    everyone(greet)

    pieces = 4
    piece = steps // pieces
    load_series = [pltpu.make_async_copy(series.at[k], inputs.at[k], load_sem.at[k]) for k in range(samples)]
    load_embed = [
        pltpu.make_async_copy(
            w_embed.at[pl.ds(k * piece, piece), :], embed.at[pl.ds(k * piece, piece), :],
            load_sem.at[samples + k],
        )
        for k in range(pieces)
    ]
    base = samples + pieces
    load_rest = [
        pltpu.make_async_copy(src, dst, load_sem.at[base + k])
        for k, (src, dst) in enumerate([
            (w_query, wq.at[t]), (w_key, wk.at[t]), (w_value, wv.at[t]), (w_out, wo.at[t]),
            (w_head, wh.at[t]), (target.at[t], tg.at[t]), (norm_gain, gain_row),
        ])
    ]
    for copy in load_series + load_embed + load_rest:
        copy.start()

    width = w_embed.shape[1]
    shifts = []
    for s in range(samples):
        load_series[s].wait()
        x = inputs[s].astype(F32)
        mean = jnp.mean(x, axis=1, keepdims=True)
        centred = x - mean
        spread_sum = jnp.sum(centred * centred, axis=1, keepdims=True)
        pack[s, :rows, width:width + 128] = jnp.broadcast_to(mean, (rows, 128))
        pack[s, :rows, width + 128:] = jnp.broadcast_to(spread_sum, (rows, 128))
        pack[s, rows:, width:] = jnp.zeros((8, 256), F32)
        shifts.append(centred.astype(BF16))
    shifts.append(jnp.ones((16, steps), BF16))
    left = jnp.concatenate(shifts, axis=0)
    total = None
    for k in range(pieces):
        load_embed[k].wait()
        cols = slice(k * piece, (k + 1) * piece)
        part = dot(left[:, cols], embed[cols, :])
        total = part if total is None else total + part
    for s in range(samples):
        pack[s, :rows, :width] = total[s * rows:(s + 1) * rows]
        pack[s, rows:, :width] = total[samples * rows:samples * rows + 8]

    pl.semaphore_wait(barrier, 2 * n - 1)
    first = to_pair(0, pack.at[other], got)
    first.start()
    weight_copies = [
        to_pair(1, w_query, wq.at[t]),
        to_pair(2, w_key, wk.at[t]),
        to_pair(3, w_value, wv.at[t]),
        to_pair(4, w_out, wo.at[t]),
        to_pair(5, w_head, wh.at[t]),
        to_pair(6, target.at[other], tg.at[t]),
    ]
    for copy in weight_copies:
        copy.start()
    first.wait()

    mean_a, mean_b = pack[t, :rows, width:width + 1], got[:rows, width:width + 1]
    sq_a, sq_b = pack[t, :rows, width + 128:width + 129], got[:rows, width + 128:width + 129]
    center = (mean_a + mean_b) * 0.5
    half_gap = (mean_a - mean_b) * 0.5
    deviation = jnp.sqrt((sq_a + sq_b) * (1.0 / (2 * steps)) + half_gap * half_gap + EPSILON)
    sums_a, sums_b = pack[t, rows:rows + 1, :width], got[rows:rows + 1, :width]
    hidden = (
        (pack[t, :rows, :width] + got[:rows, :width] + half_gap * (sums_a - sums_b)) / deviation
    ).astype(BF16)
    hid[t, block, :] = hidden

    hid_from = lambda p: hid.at[t, pl.ds(pl.multiple_of(p * rows, rows), rows), :]
    spread(hid_from, hid_send, hid_recv)

    forward_blocks(hid_from, hid_send, hid_recv)
    for copy in weight_copies + load_rest:
        copy.wait()
    queries = jnp.concatenate([dot(hidden, wq[0]), dot(hidden, wq[1])], axis=1).astype(BF16)
    queries = (queries.astype(F32) * HEAD_DIM ** (-0.5)).astype(BF16)
    q_heads = [queries[:, h * HEAD_DIM:(h + 1) * HEAD_DIM] for h in range(heads)]

    settle(hid_from, hid_send, hid_recv, "recv")
    relay = to_pair(7, hid.at[t], hid.at[t])
    relay.start()

    chunks = n * rows // key_chunk

    def chunk_rows(c):
        if chunks == 1:
            return pl.ds(0, key_chunk)
        return pl.ds(pl.multiple_of(c * key_chunk, key_chunk), key_chunk)

    def forward(c, carry):
        totals, summed = carry
        at = chunk_rows(c)
        h_rows = hid[t, at, :]
        key_rows = jnp.concatenate([dot(h_rows, wk[0]), dot(h_rows, wk[1])], axis=1).astype(BF16)
        value_rows = jnp.concatenate([dot(h_rows, wv[0]), dot(h_rows, wv[1])], axis=1).astype(BF16)
        keys[at, :] = key_rows
        values[at, :] = value_rows
        new_totals, new_summed = [], []
        for h in range(heads):
            cols = slice(h * HEAD_DIM, (h + 1) * HEAD_DIM)
            p = jnp.exp(dot_nt(q_heads[h], key_rows[:, cols]))
            powers[h, c] = p
            new_totals.append(totals[h] + jnp.sum(p, axis=1, keepdims=True))
            new_summed.append(summed[h] + dot(p.astype(BF16), value_rows[:, cols]))
        return tuple(new_totals), tuple(new_summed)

    zero = (
        tuple(jnp.zeros((rows, 1), F32) for _ in range(heads)),
        tuple(jnp.zeros((rows, HEAD_DIM), F32) for _ in range(heads)),
    )
    totals, summed = repeat(chunks, forward, zero)
    context = jnp.concatenate([summed[h] / totals[h] for h in range(heads)], axis=1)
    context_low = context.astype(BF16)
    half = context.shape[1] // 2
    w_out_all = wo[...].reshape(2 * half, width)
    residual = hidden.astype(F32) + dot(context_low, w_out_all)
    shifted = residual - jnp.mean(residual, axis=1, keepdims=True)
    norm_root = jnp.sqrt(jnp.mean(shifted * shifted, axis=1, keepdims=True) + EPSILON)
    unit_rows = shifted / norm_root
    gain = gain_row[...]
    normal_out = (unit_rows * gain).astype(BF16)
    no2[t] = normal_out
    send_no = to_pair(8, no2.at[t], no2.at[t])
    send_no.start()
    grad_normal = jnp.zeros((rows, width), F32)
    for h in range(2):
        horizon_norm = dot(normal_out, wh[h])
        pred_half[h] = horizon_norm * deviation + center
        errors = horizon_norm - (tg[h] - center) / deviation
        grad_h = (errors * (2.0 / (samples * horizon))).astype(BF16)
        gh_all[h] = grad_h
        grad_normal += dot_nt(grad_h, wh[h])
    send_gh = to_pair(9, gh_all.at[other], gh2.at[t])
    send_gh.start()
    send_pred = to_pair(10, pred_half.at[other], pred_got)
    send_pred.start()
    gh2[t] = gh_all[t]
    pred_out[t] = pred_half[t]

    gain_mine[...] = jnp.sum(grad_normal * unit_rows, axis=0, keepdims=True)
    grad_unit = grad_normal * gain
    grad_mix = (
        (
            grad_unit
            - jnp.mean(grad_unit, axis=1, keepdims=True)
            - unit_rows * jnp.mean(grad_unit * unit_rows, axis=1, keepdims=True)
        )
        / norm_root
    ).astype(BF16)
    gm2[t] = grad_mix
    for h in range(2):
        cl_all[h] = context_low[:, h * half:(h + 1) * half]
    send_gm = to_pair(11, gm2.at[t], gm2.at[t])
    send_gm.start()
    send_cl = to_pair(12, cl_all.at[other], cl2.at[t])
    send_cl.start()
    cl2[t] = cl_all[t]

    def gain_copy(where, p, q, slot):
        return pltpu.make_async_remote_copy(
            src_ref=gain_mine, dst_ref=gains.at[slot], send_sem=gain_send.at[where], recv_sem=gain_recv.at[slot],
            device_id={"var": p, "tm": q}, device_id_type=MESH,
        )

    if reduce_here:
        gains[my_id] = gain_mine[...]
        everyone(lambda where, p, q: gain_copy(where, p, q, my_id).start())
    else:
        gain_out[...] = gain_mine[...]

    send_no.wait()
    send_gh.wait()
    head_term = dot_tn(no2[...].reshape(samples * rows, width), gh2[...].reshape(samples * rows, horizon // 2))
    if reduce_here:
        by_lo = head_term.reshape(n_hi, 2, width // n, horizon // 2)
        for k in range(2):
            head_term_f[k] = by_lo[:, k]
            head_src[k] = by_lo[:, k].astype(BF16)
        head_first = near_copy(head_src, head_near, hr_send, hr_recv)
        head_first.start()
    else:
        head_out[...] = head_term
    grad_context = dot_nt(grad_mix, w_out_all)
    gc_heads, row_dots, scales = [], [], []
    for h in range(heads):
        cols = slice(h * HEAD_DIM, (h + 1) * HEAD_DIM)
        gc_heads.append(grad_context[:, cols].astype(BF16))
        row_dots.append(jnp.sum(grad_context[:, cols] * context[:, cols], axis=1, keepdims=True))
        scales.append(1.0 / totals[h])

    def backward(c, carry):
        at = chunk_rows(c)
        key_rows, value_rows = keys[at, :], values[at, :]
        results = []
        for h in range(heads):
            cols = slice(h * HEAD_DIM, (h + 1) * HEAD_DIM)
            grad_weights = dot_nt(gc_heads[h], value_rows[:, cols])
            grad_scores = (powers[h, c] * scales[h] * (grad_weights - row_dots[h])).astype(BF16)
            results.append(carry[h] + dot(grad_scores, key_rows[:, cols]))
        return tuple(results)

    grads = repeat(chunks, backward, zero[1])
    grad_query = (jnp.concatenate(grads, axis=1) * HEAD_DIM ** (-0.5)).astype(BF16)
    for h in range(2):
        gq_src[h] = grad_query[:, h * half:(h + 1) * half]

    swap = to_pair(13, gq_src.at[other], gq_all.at[t, block, :])
    swap.start()
    gq_all[t, block, :] = gq_src[t]
    gq_from = lambda p: gq_all.at[:, pl.ds(pl.multiple_of(p * rows, rows), rows), :]

    if reduce_here:
        head_first.wait()
        line_sum(head_term_f, head_near, head_sum, head_slots, hr_send, hr_recv)
    send_gm.wait()
    send_cl.wait()
    out_term = dot_tn(cl2[...].reshape(samples * rows, half), gm2[...].reshape(samples * rows, width))
    swap.wait()
    spread(gq_from, gq_send, gq_recv)
    if reduce_here:
        by_lo = out_term.reshape(n_hi, 2, half // n, width)
        for k in range(2):
            out_term_f[k] = by_lo[:, k]
            out_src[k] = by_lo[:, k].astype(BF16)
        out_first = near_copy(out_src, out_near, or_send, or_recv)
        out_first.start()
    else:
        final_out[...] = out_term
    send_pred.wait()
    pred_out[other] = pred_got[...]
    relay.wait()
    forward_blocks(gq_from, gq_send, gq_recv)
    head_from = lambda p: head_full.at[p]
    out_from = lambda p: out_full.at[p]

    if reduce_here:
        out_first.wait()
        line_sum(out_term_f, out_near, out_sum, out_slots, or_send, or_recv)
        line_wait(head_sum, head_slots, hr_send, hr_recv, "recv")
        head_full[me] = jnp.sum(head_slots[...].astype(F32), axis=0).astype(BF16)
        spread(head_from, ha_send, ha_recv)
        line_wait(out_sum, out_slots, or_send, or_recv, "recv")
        out_full[me] = jnp.sum(out_slots[...].astype(F32), axis=0).astype(BF16)
        spread(out_from, oa_send, oa_recv)

    settle(gq_from, gq_send, gq_recv, "recv")
    query_out[...] = dot_tn(
        gq_all[...].reshape(samples * n * rows, half), hid[...].reshape(samples * n * rows, width)
    ).T
    if reduce_here:
        forward_blocks(head_from, ha_send, ha_recv)
        forward_blocks(out_from, oa_send, oa_recv)
        everyone(lambda where, p, q: gain_copy(where, p, q, where).wait_recv())
        gain_out[...] = jnp.sum(gains[...], axis=0)
        settle(head_from, ha_send, ha_recv, "recv")
        head_out[...] = head_full[...].reshape(head_out.shape)
        settle(out_from, oa_send, oa_recv, "recv")
        final_out[...] = out_full[...].astype(F32).reshape(final_out.shape)

    settle(hid_from, hid_send, hid_recv, "send")
    settle(gq_from, gq_send, gq_recv, "send")
    if reduce_here:
        everyone(lambda where, p, q: gain_copy(where, p, q, my_id).wait_send())
        line_wait(head_sum, head_slots, hr_send, hr_recv, "send")
        line_wait(out_sum, out_slots, or_send, or_recv, "send")
        settle(head_from, ha_send, ha_recv, "send")
        settle(out_from, oa_send, oa_recv, "send")


def deliver(*refs):
    count = (len(refs) - 4) // 3
    sources, results, held = refs[:count], refs[count:2 * count], refs[2 * count:3 * count]
    turned, in_sems, out_sems, turned_sem = refs[3 * count:]
    arrive = [pltpu.make_async_copy(sources[k], held[k], in_sems.at[k]) for k in range(count)]
    leave = [pltpu.make_async_copy(held[k], results[k], out_sems.at[k]) for k in range(count - 1)]
    for copy in arrive:
        copy.start()
    for k in range(count - 1):
        arrive[k].wait()
        leave[k].start()
    arrive[count - 1].wait()
    turned[...] = held[count - 1][...].astype(F32).T
    last = pltpu.make_async_copy(turned, results[count - 1], turned_sem)
    last.start()
    for copy in leave + [last]:
        copy.wait()


def solution(mesh):
    n = mesh.shape["var"]

    def per_device(series, target, w_embed, w_query, w_key, w_value, w_out, norm_gain, w_head):
        samples, rows, steps = series.shape
        width = w_embed.shape[1]
        half = w_query.shape[1]
        hor = target.shape[2]
        heads = 2 * half // HEAD_DIM
        key_chunk = min(512, n * rows)
        chunks = n * rows // key_chunk
        reduce_here = width % (16 * n) == 0 and half % (16 * n) == 0
        cuts = n if reduce_here else 1
        line = n // 2 if reduce_here else 1
        v = pltpu.VMEM
        dma = pltpu.SemaphoreType.DMA
        outs = pl.pallas_call(
            functools.partial(kernel, n, reduce_here, key_chunk),
            out_shape=(
                jax.ShapeDtypeStruct((samples, rows, hor), F32),
                jax.ShapeDtypeStruct((width, half), F32),
                jax.ShapeDtypeStruct((half, width), F32),
                jax.ShapeDtypeStruct((1, width), F32),
                jax.ShapeDtypeStruct((width, hor), BF16 if reduce_here else F32),
            ),
            in_specs=[pl.BlockSpec(memory_space=pltpu.HBM)] * 8 + [pl.BlockSpec(memory_space=pltpu.VMEM)],
            out_specs=[pl.BlockSpec(memory_space=pltpu.VMEM)] * 5,
            scratch_shapes=[
                v((samples, rows + 8, width + 256), F32),
                v((rows + 8, width + 256), F32),
                v((2, width, half), BF16),
                v((2, width, half), BF16),
                v((2, width, half), BF16),
                v((2, half, width), BF16),
                v((2, width, hor), BF16),
                v((2, rows, hor), F32),
                v((samples, n * rows, width), BF16),
                v((n * rows, 2 * half), BF16),
                v((n * rows, 2 * half), BF16),
                v((heads, chunks, rows, key_chunk), F32),
                v((2, rows, hor), F32),
                v((rows, hor), F32),
                v((samples, rows, width), BF16),
                v((2, rows, hor), BF16),
                v((samples, rows, hor), BF16),
                v((samples, rows, width), BF16),
                v((2, rows, half), BF16),
                v((samples, rows, half), BF16),
                v((2, rows, half), BF16),
                v((samples, n * rows, half), BF16),
                v((2 * cuts, 1, width), F32),
                v((1, width), F32),
                v((2, line, width // cuts, hor), BF16),
                v((line, width // cuts, hor), BF16),
                v((cuts, width // cuts, hor), BF16),
                v((2, line, half // cuts, width), BF16),
                v((line, half // cuts, width), BF16),
                v((cuts, half // cuts, width), BF16),
                dma((14,)), dma((14,)),
                dma((n,)), dma((n,)),
                dma((n,)), dma((n,)),
                dma((2 * n,)), dma((2 * n,)),
                dma((n,)), dma((n,)), dma((n,)), dma((n,)),
                dma((n,)), dma((n,)), dma((n,)), dma((n,)),
                v((samples, rows, steps), BF16),
                v((steps, width), BF16),
                v((2, line, width // cuts, hor), F32),
                v((line, width // cuts, hor), BF16),
                v((line, width // cuts, hor), BF16),
                v((2, line, half // cuts, width), F32),
                v((line, half // cuts, width), BF16),
                v((line, half // cuts, width), BF16),
                v((1, width), F32),
                dma((samples + 11,)),
            ],
            compiler_params=pltpu.CompilerParams(
                collective_id=0,
                has_side_effects=True,
                vmem_limit_bytes=VMEM_GRANT,
            ),
        )(series, target, w_embed, w_query, w_key, w_value, w_out, norm_gain.reshape(1, width), w_head)
        pred, query, final, gain, head = outs
        if not reduce_here:
            final, gain, head = lax.psum((final, gain, head), "var")
            gain = lax.psum(gain, "tm")
            return pred, query, final, gain.reshape(width), head
        plain = (pred, query, final, gain, head)
        shapes = [jax.ShapeDtypeStruct(x.shape, x.dtype) for x in plain[:4]]
        shapes.append(jax.ShapeDtypeStruct((hor, width), F32))
        pred, query, final, gain, head = pl.pallas_call(
            deliver,
            out_shape=tuple(shapes),
            in_specs=[pl.BlockSpec(memory_space=pltpu.HBM)] * 5,
            out_specs=[pl.BlockSpec(memory_space=pltpu.HBM)] * 5,
            scratch_shapes=[v(x.shape, x.dtype) for x in plain]
            + [v((hor, width), F32), dma((5,)), dma((4,)), dma(())],
            compiler_params=pltpu.CompilerParams(vmem_limit_bytes=VMEM_GRANT),
        )(*plain)
        return pred, query, final, gain.reshape(width), jnp.transpose(head)

    in_specs = (
        P("groups", "var", "tm"),
        P("groups", "var", "tm"),
        P("tm", None),
        P(None, "tm"),
        P(None, "tm"),
        P(None, "tm"),
        P("tm", None),
        P(),
        P(None, "tm"),
    )
    out_specs = (
        P("groups", "var", "tm"),
        P("groups", "tm"),
        P(("groups", "tm"), None),
        P("groups"),
        P("groups", "tm"),
    )
    return jax.shard_map(
        per_device, mesh=mesh, in_specs=in_specs, out_specs=out_specs, check_vma=False
    )
```
